128 devices in a mesh: owner: 16 (over z, y), group: 8 (over x, core).
Axes of the slice: x: 4, y: 4, z: 4, core: 2. Of those that a mesh axis runs over, the one named last changes fastest.
Arguments:
- memory: bfloat16 [262144, 512], P(('owner', 'group')), may hold values from -64 to 64
- touched: int32 [128, 128, 4], P(('owner', 'group')), may hold values from 0 to 2047
- src_pos: int32 [65536], P(('owner', 'group')), may hold values from 0 to 511
- dst_owner: int32 [65536, 1], P(('owner', 'group')), may hold values from 0 to 127; in each aligned block of 512 rows (0 to 511, 512 to 1023, ...) at most 8 rows name the same one
- dst_slot: int32 [65536], P(('owner', 'group')), may hold values from 0 to 3
- neighbors: int32 [65536, 16], P(('owner', 'group')), may hold values from 0 to 511
- ev_time: int32 [65536], P(('owner', 'group')), may hold values from 0 to 4095
- neigh_time: int32 [65536, 16], P(('owner', 'group')), may hold values from 0 to 4095
- time_freq: float32 [128], replicated, may hold values from 0.001 to 0.5
- w_query: bfloat16 [512, 512], replicated, may hold values from -0.25 to 0.25
- w_key: bfloat16 [640, 512], replicated, may hold values from -0.25 to 0.25
- w_value: bfloat16 [640, 512], replicated, may hold values from -0.25 to 0.25
- w_out: bfloat16 [512, 512], replicated, may hold values from -0.25 to 0.25
- w_msg1: bfloat16 [1152, 1024], replicated, may hold values from -0.1875 to 0.1875
- w_msg2: bfloat16 [1024, 1024], replicated, may hold values from -0.1875 to 0.1875
- w_input: bfloat16 [1024, 1536], replicated, may hold values from -0.1875 to 0.1875
- w_hidden: bfloat16 [512, 1536], replicated, may hold values from -0.25 to 0.25
Outputs:
- embeddings: bfloat16 [65536, 512], P(('owner', 'group'))
- new_memory: bfloat16 [262144, 512], P(('owner', 'group'))
The draws below stay inside these ranges and needn't reach their ends.
Inputs may be any that keep to these rules, and one draw needn't show every extreme that they name: `dst_owner`: events of one device (aligned blocks of 512) name one owner at most 8 times; some owner is named exactly 8 times.
All inputs are finite; a program needn't handle non-finite values.
Results may differ from the reference program's by a relative error of at most 0.0043.
Values may be sent and summed in bfloat16 or wider, within the bound.
A program may use at most 128 MiB of HBM per device.

```python
import math
import jax
import jax.numpy as jnp
import numpy as np
from jax import lax

M = 512
MSG = 1024
TE = 128
HEADS = 2
NEIGH = 16
SLOTS = 4
NB = 4096
NODE_DEV = 2048
EV_DEV = 512
CAP = 8
T_DEV = 512
EVENTS = 65536
NODES = 262144
DEVICES = 128


def draw_memory(key, part):
    key = jax.random.fold_in(key, 11)
    first, second = jax.random.split(key)
    base = jnp.clip(jax.random.normal(first, (NODES, M), jnp.float32), -6.0, 6.0)
    scale = jnp.exp(jax.random.uniform(second, (NODES, 1), jnp.float32, 0.0, math.log(10.0)))
    return (base * scale).astype(jnp.bfloat16)


def set_ends(entries, own_key, least, top_value):
    shape = entries.shape
    index_at = [jax.random.randint(jax.random.fold_in(own_key, axis), (), 0, shape[axis]) for axis in range(len(shape))]
    entries = entries.at[tuple(index_at)].set(least)
    longest = shape.index(max(shape))
    index_at[longest] = (index_at[longest] + 1) % shape[longest]
    return entries.at[tuple(index_at)].set(top_value)


def assign_block(stream_key, own, number, rows, number_of, top, bound, lean):
    ranking = jax.random.permutation(stream_key, number_of)
    crowded, usual = portions_of(number_of, rows * top, bound, lean, True), portions_of(number_of, rows * top, bound, lean, False)
    places = jnp.arange(number_of)

    def named(lengths, rotation):
        used = int((lengths > 0).sum())
        fixed = max(1, used // 4)
        shifted = fixed + (places - fixed + rotation * (used - fixed)) % max(1, number_of - fixed)
        return jnp.zeros((number_of,), jnp.int32).at[ranking[jnp.where(places < fixed, places, shifted)]].set(jnp.asarray(lengths, jnp.int32))

    lengths = jnp.where(number % 4 == 0, named(crowded, number // 4), named(usual, number - number // 4 - 1))
    mixed = jax.random.permutation(jax.random.fold_in(own, 3), number_of)
    giver, taker = mixed[0:number_of // 2 * 2:2], mixed[1:number_of // 2 * 2:2]
    slack = jnp.minimum(lengths[giver] - 1, bound - lengths[taker]) // 2
    slack = jnp.where((giver == ranking[0]) | (taker == ranking[0]) | (lengths[taker] == 0), 0, jnp.maximum(slack, 0))
    shifted = jax.random.randint(jax.random.fold_in(own, 4), (number_of // 2,), 0, 1 << 20) % (slack + 1)
    lengths = lengths.at[giver].add(-shifted).at[taker].add(shifted)
    items = jnp.searchsorted(jnp.cumsum(lengths), jnp.arange(rows * top), side="right").astype(jnp.int32)
    listing = items.reshape(top, rows).T
    listing = listing[jax.random.permutation(jax.random.fold_in(own, 1), rows)]
    rotation = jax.random.randint(jax.random.fold_in(own, 2), (rows, 1), 0, top)
    return jnp.take_along_axis(listing, (jnp.arange(top)[None, :] + rotation) % top, axis=1)


def portions_of(number_of, total, most, slope, full):
    portions = [(1 << 20) // math.isqrt(grade ** slope) + 1 for grade in range(1, number_of + 1)]
    largest = most if full else min(most, max(-(-total // number_of), total * portions[0] // sum(portions)))
    least = 1 if total - largest >= number_of - 1 else 0
    given, spare = [largest] + [least] * (number_of - 1), total - largest - least * (number_of - 1)
    while spare > 0:
        free = [i for i in range(1, number_of) if given[i] < largest] or [i for i in range(1, number_of) if given[i] < most]
        mass, budget = sum([portions[i] for i in free]), spare
        for i in free:
            extra = min(most - given[i], max(1, budget * portions[i] // mass), spare)
            given[i] = given[i] + extra
            spare = spare - extra
    return np.array(given)


def scatter_about(rng, extent, deviation, bound, kind=jnp.bfloat16):
    result = deviation * jax.random.normal(rng, extent, jnp.float32)
    return jnp.clip(result, min=-bound, max=bound).astype(kind)


def setup_inputs(seed: int = 0) -> dict:
    seeds = jax.random.split(jax.random.key(seed), 18)
    memory = draw_memory(jax.random.fold_in(seeds[17], 71), 0)
    touched = set_ends(jax.random.randint(seeds[1], (DEVICES, DEVICES, SLOTS), 0, NODE_DEV), jax.random.fold_in(seeds[1], 1), 0, NODE_DEV - 1).astype(jnp.int32)
    src_pos = set_ends(jax.random.randint(seeds[2], (EVENTS,), 0, T_DEV), jax.random.fold_in(seeds[2], 1), 0, T_DEV - 1).astype(jnp.int32)
    dst_owner_keys = jax.random.split(jax.random.fold_in(seeds[3], 1), EVENTS // EV_DEV)
    dst_owner_turns = jax.random.permutation(jax.random.fold_in(seeds[3], 3), EVENTS // EV_DEV)
    dst_owner = jax.vmap(lambda own, number: assign_block(jax.random.fold_in(seeds[3], 2), own, number, EV_DEV, DEVICES, 1, CAP, 2))(dst_owner_keys, dst_owner_turns).reshape((EVENTS, 1))
    dst_slot = set_ends(jax.random.randint(seeds[4], (EVENTS,), 0, SLOTS), jax.random.fold_in(seeds[4], 1), 0, SLOTS - 1).astype(jnp.int32)
    neighbors = set_ends(jax.random.randint(seeds[5], (EVENTS, NEIGH), 0, T_DEV), jax.random.fold_in(seeds[5], 1), 0, T_DEV - 1).astype(jnp.int32)
    ev_time = set_ends(jax.random.randint(seeds[6], (EVENTS,), 0, NB), jax.random.fold_in(seeds[6], 1), 0, NB - 1).astype(jnp.int32)
    neigh_time = set_ends(jax.random.randint(seeds[7], (EVENTS, NEIGH), 0, NB), jax.random.fold_in(seeds[7], 1), 0, NB - 1).astype(jnp.int32)
    time_freq = jnp.clip(jnp.exp(jax.random.uniform(seeds[8], (TE,), jnp.float32, math.log(0.001), math.log(0.5))), 0.001, 0.5)
    w_query = scatter_about(seeds[9], (M, M), M ** -0.5, 0.25)
    w_key = scatter_about(seeds[10], (M + TE, M), (M + TE) ** -0.5, 0.25)
    w_value = scatter_about(seeds[11], (M + TE, M), (M + TE) ** -0.5, 0.25)
    w_out = scatter_about(seeds[12], (M, M), M ** -0.5, 0.25)
    w_msg1 = scatter_about(seeds[13], (2 * M + TE, MSG), (2 * M + TE) ** -0.5, 0.1875)
    w_msg2 = scatter_about(seeds[14], (MSG, MSG), MSG ** -0.5, 0.1875)
    w_input = scatter_about(seeds[15], (MSG, 3 * M), MSG ** -0.5, 0.1875)
    w_hidden = scatter_about(seeds[16], (M, 3 * M), M ** -0.5, 0.25)
    return {"memory": memory, "touched": touched, "src_pos": src_pos, "dst_owner": dst_owner, "dst_slot": dst_slot, "neighbors": neighbors, "ev_time": ev_time, "neigh_time": neigh_time, "time_freq": time_freq, "w_query": w_query, "w_key": w_key, "w_value": w_value, "w_out": w_out, "w_msg1": w_msg1, "w_msg2": w_msg2, "w_input": w_input, "w_hidden": w_hidden}


def time_code(delta, time_freq):
    return jnp.cos(delta.astype(jnp.float32)[..., None] * time_freq).astype(jnp.bfloat16)

def event_block(table, src_pos, dst_pos, neighbors, ev_time, neigh_time, time_freq, w_query, w_key, w_value, w_out, w_msg1, w_msg2):
    count = src_pos.shape[0]
    src_mem = table[src_pos]
    dst_mem = table[dst_pos]
    query = jnp.dot(dst_mem, w_query, preferred_element_type=jnp.float32)
    key_table = jnp.dot(table, w_key[:M], preferred_element_type=jnp.float32)
    value_table = jnp.dot(table, w_value[:M], preferred_element_type=jnp.float32)
    pair_code = time_code(ev_time[:, None] - neigh_time, time_freq).reshape(-1, TE)
    keys = key_table[neighbors] + jnp.dot(pair_code, w_key[M:], preferred_element_type=jnp.float32).reshape(count, NEIGH, M)
    values = value_table[neighbors] + jnp.dot(pair_code, w_value[M:], preferred_element_type=jnp.float32).reshape(count, NEIGH, M)
    head_q = query.reshape(count, HEADS, M // HEADS)
    head_k = keys.reshape(count, NEIGH, HEADS, M // HEADS)
    head_v = values.reshape(count, NEIGH, HEADS, M // HEADS)
    scores = jnp.einsum('ehd,ekhd->ehk', head_q, head_k) / jnp.sqrt(jnp.float32(M // HEADS))
    weights = jax.nn.softmax(scores, axis=-1)
    att = jnp.einsum('ehk,ekhd->ehd', weights, head_v).reshape(count, M).astype(jnp.bfloat16)
    emb = (dst_mem.astype(jnp.float32) + jnp.dot(att, w_out, preferred_element_type=jnp.float32)).astype(jnp.bfloat16)
    joined = jnp.concatenate([src_mem, emb, time_code(ev_time, time_freq)], axis=1)
    hidden = jax.nn.relu(jnp.dot(joined, w_msg1, preferred_element_type=jnp.float32)).astype(jnp.bfloat16)
    message = jnp.dot(hidden, w_msg2, preferred_element_type=jnp.float32).astype(jnp.bfloat16)
    return (emb, message)

def gru_update(agg, old, w_input, w_hidden):
    gate_in = jnp.dot(agg, w_input, preferred_element_type=jnp.float32)
    gate_state = jnp.dot(old, w_hidden, preferred_element_type=jnp.float32)
    reset = jax.nn.sigmoid(gate_in[:, :M] + gate_state[:, :M])
    update = jax.nn.sigmoid(gate_in[:, M:2 * M] + gate_state[:, M:2 * M])
    candidate = jnp.tanh(gate_in[:, 2 * M:] + reset * gate_state[:, 2 * M:])
    return ((1.0 - update) * candidate + update * old.astype(jnp.float32)).astype(jnp.bfloat16)

def block_partial(items):
    nodes, block_msg = items
    same = nodes[:, None] == nodes[None, :]
    part = jnp.dot(same.astype(jnp.bfloat16), block_msg, preferred_element_type=jnp.float32).astype(jnp.bfloat16)
    index = jnp.arange(EV_DEV, dtype=jnp.int32)
    earlier = lax.optimization_barrier(jnp.sum((same & (index[None, :] < index[:, None])).astype(jnp.int32), axis=1))
    leader = (earlier == 0).astype(jnp.float32)
    return part.astype(jnp.float32) * leader[:, None]

def reference(memory, touched, src_pos, dst_owner, dst_slot, neighbors, ev_time, neigh_time, time_freq, w_query, w_key, w_value, w_out, w_msg1, w_msg2, w_input, w_hidden):
    base = (jnp.arange(DEVICES, dtype=jnp.int32) * NODE_DEV)[None, :, None]
    rows = (touched + base).reshape(DEVICES, DEVICES * SLOTS)
    dst_pos = dst_owner[:, 0] * SLOTS + dst_slot

    def one_block(items):
        block_rows, s_pos, d_pos, nbrs, e_time, n_time = items
        table = memory[block_rows]
        return event_block(table, s_pos, d_pos, nbrs, e_time, n_time, time_freq, w_query, w_key, w_value, w_out, w_msg1, w_msg2)
    emb, message = lax.map(one_block, (rows, src_pos.reshape(DEVICES, EV_DEV), dst_pos.reshape(DEVICES, EV_DEV), neighbors.reshape(DEVICES, EV_DEV, NEIGH), ev_time.reshape(DEVICES, EV_DEV), neigh_time.reshape(DEVICES, EV_DEV, NEIGH)))
    emb = emb.reshape(EVENTS, M)
    dst_node = jnp.take_along_axis(rows, dst_pos.reshape(DEVICES, EV_DEV), axis=1).reshape(EVENTS).astype(jnp.int32)
    partial_value = lax.map(block_partial, (dst_node.reshape(DEVICES, EV_DEV), message)).reshape(EVENTS, MSG)
    order = jnp.argsort(dst_node, stable=True).astype(jnp.int32)
    sorted_ids = dst_node[order]
    flags = jnp.concatenate([jnp.ones((1,), jnp.int32), (sorted_ids[1:] != sorted_ids[:-1]).astype(jnp.int32)])
    segment = (jnp.cumsum(flags) - 1).astype(jnp.int32)
    sums = jax.ops.segment_sum(partial_value[order], segment, num_segments=EVENTS)
    counts = jax.ops.segment_sum(jnp.ones((EVENTS,), jnp.float32), segment, num_segments=EVENTS)
    agg_sorted = sums[segment] / counts[segment][:, None]
    agg = jnp.zeros((EVENTS, MSG), jnp.float32).at[order].set(agg_sorted).astype(jnp.bfloat16)

    def one_update(items):
        block_agg, block_nodes = items
        return gru_update(block_agg, memory[block_nodes], w_input, w_hidden)
    fresh = lax.map(one_update, (agg.reshape(DEVICES, EV_DEV, MSG), dst_node.reshape(DEVICES, EV_DEV)))
    new_memory = memory.at[dst_node].set(fresh.reshape(EVENTS, M))
    return (emb, new_memory)
```

```python
import functools

import jax
import jax.numpy as jnp
from jax import lax
from jax.experimental import pallas as pl
from jax.experimental.pallas import tpu as pltpu
from jax.sharding import PartitionSpec as P

HEADS = 2
MESH = pl.DeviceIdType.MESH


def swap_kernel(x_ref, o_ref, send_sem, recv_sem, local_sem):
    groups = lax.axis_size("group")
    n = lax.axis_size("owner") * groups
    me = lax.axis_index("owner") * groups + lax.axis_index("group")
    barrier = pltpu.get_barrier_semaphore()

    def place(step):
        target = lax.rem(me + step, n)
        return target, (target // groups, lax.rem(target, groups))

    def greet(step, carry):
        _, device = place(step)
        pl.semaphore_signal(barrier, inc=1, device_id=device, device_id_type=MESH)
        return carry

    lax.fori_loop(1, n, greet, 0)
    pl.semaphore_wait(barrier, n - 1)
    own = pltpu.make_async_copy(x_ref.at[me], o_ref.at[me], local_sem)
    own.start()

    def send(step, carry):
        target, device = place(step)
        pltpu.make_async_remote_copy(
            src_ref=x_ref.at[target],
            dst_ref=o_ref.at[me],
            send_sem=send_sem,
            recv_sem=recv_sem,
            device_id=device,
            device_id_type=MESH,
        ).start()
        return carry

    lax.fori_loop(1, n, send, 0)
    own.wait()
    _, device = place(1)
    pltpu.make_async_remote_copy(
        src_ref=x_ref.at[pl.ds(0, n - 1)],
        dst_ref=o_ref.at[pl.ds(0, n - 1)],
        send_sem=send_sem,
        recv_sem=recv_sem,
        device_id=device,
        device_id_type=MESH,
    ).wait()


def swap(x, number):
    return pl.pallas_call(
        swap_kernel,
        out_shape=jax.ShapeDtypeStruct(x.shape, x.dtype),
        in_specs=[pl.BlockSpec(memory_space=pltpu.VMEM)],
        out_specs=pl.BlockSpec(memory_space=pltpu.VMEM),
        scratch_shapes=[pltpu.SemaphoreType.DMA] * 3,
        compiler_params=pltpu.CompilerParams(
            collective_id=number, has_side_effects=True, vmem_limit_bytes=16 << 20
        ),
    )(x)


def dot(a, b):
    return jnp.dot(a, b, preferred_element_type=jnp.float32)


def onehot(index, size):
    return (index[:, None] == jnp.arange(size, dtype=jnp.int32)[None, :]).astype(jnp.bfloat16)


def time_code(delta, time_freq):
    return jnp.cos(delta.astype(jnp.float32)[..., None] * time_freq).astype(jnp.bfloat16)


def per_device(
    memory,
    touched,
    src_pos,
    dst_owner,
    dst_slot,
    neighbors,
    ev_time,
    neigh_time,
    time_freq,
    w_query,
    w_key,
    w_value,
    w_out,
    w_msg1,
    w_msg2,
    w_input,
    w_hidden,
):
    devices = lax.axis_size(("owner", "group"))
    node_rows, width = memory.shape
    slots = touched.shape[2]
    msg_width = w_msg2.shape[1]
    count, neigh = neighbors.shape
    head_size = width // HEADS
    positions = devices * slots
    highest = lax.Precision.HIGHEST
    target = dst_owner[:, 0]
    dst_pos = target * slots + dst_slot
    dst_hot = onehot(dst_pos, positions)
    counts = jnp.sum(dst_hot.astype(jnp.float32), axis=0).astype(jnp.int32)
    note = jnp.concatenate(
        [
            touched.reshape(devices, slots),
            counts.reshape(devices, slots),
            jnp.zeros((devices, 128 - 2 * slots), jnp.int32),
        ],
        axis=1,
    )
    notes = swap(note.reshape(devices, 1, 128), 0)[:, 0, :]
    asked = notes[:, :slots].T.reshape(-1)
    asked_count = notes[:, slots : 2 * slots].T.reshape(-1)
    picked = dot(onehot(asked, node_rows), memory).astype(jnp.bfloat16)
    outgoing = picked.reshape(slots, devices, width // 128, 128).transpose(1, 0, 2, 3)
    table = swap(outgoing.reshape(devices, slots * width // 128, 128), 1)
    table = table.reshape(positions, width)

    src_mem = dot(onehot(src_pos, positions), table).astype(jnp.bfloat16)
    dst_mem = dot(dst_hot, table).astype(jnp.bfloat16)
    query = dot(dst_mem, w_query)
    key_table = dot(table, w_key[:width])
    value_table = dot(table, w_value[:width])
    code = time_code(ev_time[None, :] - neigh_time.T, time_freq)
    head_q = query.reshape(count, HEADS, head_size)
    head_k = key_table.reshape(positions, HEADS, head_size)
    head_v = value_table.reshape(positions, HEADS, head_size)
    full = jnp.einsum("ehd,phd->hep", head_q, head_k, precision=highest)
    key_code = w_key[width:].astype(jnp.float32).reshape(-1, HEADS, head_size)
    query_code = jnp.einsum("ehd,thd->eht", head_q, key_code, precision=highest)
    scores = []
    for k in range(neigh):
        hit = neighbors[:, k][:, None] == jnp.arange(positions, dtype=jnp.int32)[None, :]
        scores.append(
            jnp.sum(jnp.where(hit[None], full, 0.0), axis=2)
            + jnp.sum(query_code * code[k].astype(jnp.float32)[:, None, :], axis=2).T
        )
    weights = jax.nn.softmax(jnp.stack(scores) / jnp.sqrt(jnp.float32(head_size)), axis=0)
    spread = jnp.zeros_like(full)
    mixed = jnp.zeros((HEADS, count, code.shape[2]), jnp.float32)
    for k in range(neigh):
        hit = neighbors[:, k][:, None] == jnp.arange(positions, dtype=jnp.int32)[None, :]
        spread += jnp.where(hit[None], weights[k][:, :, None], 0.0)
        mixed += weights[k][:, :, None] * code[k].astype(jnp.float32)[None]
    value_code = w_value[width:].astype(jnp.float32).reshape(-1, HEADS, head_size)
    att = jnp.einsum("hep,phd->ehd", spread, head_v, precision=highest)
    att = att + jnp.einsum("het,thd->ehd", mixed, value_code, precision=highest)
    att = att.reshape(count, width).astype(jnp.bfloat16)
    emb = (dst_mem.astype(jnp.float32) + dot(att, w_out)).astype(jnp.bfloat16)
    joined = jnp.concatenate([src_mem, emb, time_code(ev_time, time_freq)], axis=1)
    hidden = jax.nn.relu(dot(joined, w_msg1)).astype(jnp.bfloat16)
    message = dot(hidden, w_msg2).astype(jnp.bfloat16)
    partial = dot(dst_hot.T, message).astype(jnp.bfloat16)
    inbox = swap(partial.reshape(devices, slots * msg_width // 128, 128), 2)
    inbox = inbox.reshape(devices, slots, msg_width).transpose(1, 0, 2).reshape(positions, -1)

    match = asked[:, None] == asked[None, :]
    total = dot(match.astype(jnp.bfloat16), inbox)
    number = jnp.sum(jnp.where(match, asked_count[None, :], 0), axis=1)
    agg = (total / jnp.maximum(number, 1).astype(jnp.float32)[:, None]).astype(jnp.bfloat16)
    gate_in = dot(agg, w_input)
    gate_state = dot(picked, w_hidden)
    gates = jax.nn.sigmoid(gate_in[:, : 2 * width] + gate_state[:, : 2 * width])
    reset, update = gates[:, :width], gates[:, width:]
    candidate = jnp.tanh(gate_in[:, 2 * width :] + reset * gate_state[:, 2 * width :])
    fresh = ((1.0 - update) * candidate + update * picked.astype(jnp.float32)).astype(jnp.bfloat16)
    order = jnp.arange(positions)
    first = jnp.sum(match & (order[None, :] < order[:, None]), axis=1) == 0
    leader = jnp.where(first & (number > 0), asked, -1)
    place = onehot(leader, node_rows).T
    moved = dot(place, fresh).astype(jnp.bfloat16)
    hit = jnp.sum(place.astype(jnp.float32), axis=1) > 0
    return emb, jnp.where(hit[:, None], moved, memory)


def solution(mesh):
    rows = P(("owner", "group"))
    in_specs = (rows,) * 8 + (P(),) * 9
    return jax.shard_map(
        per_device, mesh=mesh, in_specs=in_specs, out_specs=(rows, rows), check_vma=False
    )
```

```python
import jax
import jax.numpy as jnp
from jax import lax
from jax.experimental import pallas as pl
from jax.experimental.pallas import tpu as pltpu
from jax.sharding import PartitionSpec as P

HEADS = 2
MESH = pl.DeviceIdType.MESH
f32, bf16, i32 = jnp.float32, jnp.bfloat16, jnp.int32
COS = (
    0.9999992251396179,
    -0.499994158744812,
    0.041659727692604065,
    -0.00138586456887424,
    2.4201255655498244e-05,
    -2.196603787751883e-07,
)
NN = (((1,), (0,)), ((), ()))
NT = (((1,), (1,)), ((), ()))


def dot(a, b, dims=NN):
    return lax.dot_general(a, b, dims, preferred_element_type=f32)


def iota(shape, axis):
    return lax.broadcasted_iota(i32, shape, axis)


def hot(mask):
    return jnp.where(mask, 1.0, 0.0).astype(bf16)


def split(x):
    high = x.astype(bf16)
    return high, (x - high.astype(f32)).astype(bf16)


def cosine(x):
    turns = jnp.floor(x * 0.15915494309189535 + 0.5)
    r = (x - turns * 6.28125) - turns * 0.0019353071795864769
    r = r * r
    y = COS[-1] * r + COS[-2]
    for c in COS[-3::-1]:
        y = y * r + c
    return y


def window_kernel(
    ints,
    cols,
    asks,
    freq_col,
    freq_row,
    memory_hbm,
    w_hidden_hbm,
    w_query_hbm,
    w_key_hbm,
    w_value_hbm,
    w_out_hbm,
    w_msg1_hbm,
    w_msg2_hbm,
    w_input_hbm,
    emb_hbm,
    fresh_out,
    leader_out,
    memory,
    w_hidden,
    w_query,
    w_key,
    w_value,
    w_out,
    w_msg1,
    w_msg2,
    w_input,
    load_sem,
    emb_sem,
    note,
    note_in,
    relay,
    notes,
    note_sem,
    own_sem,
    stage,
    outbox,
    inbox,
    table_sem,
    part_out,
    part_in,
    part_sem,
    code,
    picked,
    state,
    value_t,
    match_ref,
    share,
    ev_code,
    src_hot,
    dst_hot,
    dst_hot_t,
    table,
    full,
    query_code,
    spread_hi,
    spread_lo,
    emb,
    partial,
    gates,
):
    groups, owners = 8, 16
    n = groups * owners
    o, g = lax.axis_index("owner"), lax.axis_index("group")
    me = o * groups + g
    neigh, te, width = 16, 128, 512

    barrier = pltpu.get_barrier_semaphore()
    for step in range(1, groups):
        pl.semaphore_signal(
            barrier, inc=1, device_id=(o, (g + step) & (groups - 1)), device_id_type=MESH
        )
    for step in range(1, owners):
        pl.semaphore_signal(
            barrier, inc=1, device_id=((o + step) & (owners - 1), g), device_id_type=MESH
        )
    loads = []
    for number, (source, target) in enumerate(
        (
            (memory_hbm, memory),
            (w_hidden_hbm, w_hidden),
            (w_value_hbm, w_value),
            (w_query_hbm, w_query),
            (w_key_hbm, w_key),
            (w_out_hbm, w_out),
            (w_msg1_hbm, w_msg1),
            (w_msg2_hbm, w_msg2),
            (w_input_hbm, w_input),
        )
    ):
        load = pltpu.make_async_copy(source, target, load_sem.at[number])
        load.start()
        loads.append(load)

    row = iota((n, 1), 0)
    device = ((row & (owners - 1)) * groups) + (row // owners)
    owner_hot = hot(device == ints[34:35, :])
    slot_hot = hot(iota((n, 512), 0) == ints[35:36, :] + 4)
    note[...] = asks[...] + dot(owner_hot, slot_hot, NT).astype(i32)
    pl.semaphore_wait(barrier, groups + owners - 2)

    def note_part(index):
        return pl.ds(pl.multiple_of(index * owners, owners), owners)

    own = pltpu.make_async_copy(note.at[note_part(g)], note_in.at[note_part(g)], own_sem.at[0])
    own.start()
    for step in range(1, groups):
        peer = (g + step) & (groups - 1)
        pltpu.make_async_remote_copy(
            src_ref=note.at[note_part(peer)],
            dst_ref=note_in.at[note_part(g)],
            send_sem=note_sem.at[0],
            recv_sem=note_sem.at[1],
            device_id=(o, peer),
            device_id_type=MESH,
        ).start()

    def make_codes(first):
        def codes(i, carry):
            rows = pl.ds(pl.multiple_of(i * 16, 16), 16)
            freq = freq_col[rows, :]
            for k in range(first, first + neigh // 2):
                delta = ints[k + neigh : k + neigh + 1, :].astype(f32)
                code[k, rows, :] = cosine(freq * delta).astype(bf16).astype(f32)
            return carry

        lax.fori_loop(0, te // 16, codes, 0)

    make_codes(0)
    own.wait()
    some = (groups - 1) * owners
    pltpu.make_async_remote_copy(
        src_ref=note.at[pl.ds(0, some)],
        dst_ref=note_in.at[pl.ds(0, some)],
        send_sem=note_sem.at[0],
        recv_sem=note_sem.at[1],
        device_id=(o, (g + 1) & (groups - 1)),
        device_id_type=MESH,
    ).wait()
    for owner in range(owners):
        relay[owner] = note_in[pl.ds(owner, groups, stride=owners), :]
    own = pltpu.make_async_copy(relay.at[o], notes.at[o], own_sem.at[1])
    own.start()
    for step in range(1, owners):
        peer = (o + step) & (owners - 1)
        pltpu.make_async_remote_copy(
            src_ref=relay.at[peer],
            dst_ref=notes.at[o],
            send_sem=note_sem.at[2],
            recv_sem=note_sem.at[3],
            device_id=(peer, g),
            device_id_type=MESH,
        ).start()
    make_codes(neigh // 2)
    own.wait()
    pltpu.make_async_remote_copy(
        src_ref=relay.at[pl.ds(0, owners - 1)],
        dst_ref=notes.at[pl.ds(0, owners - 1)],
        send_sem=note_sem.at[2],
        recv_sem=note_sem.at[3],
        device_id=((o + 1) & (owners - 1), g),
        device_id_type=MESH,
    ).wait()
    known = notes[...].reshape(n, 128)
    known_t = known.astype(f32).T.astype(i32)

    loads[0].wait()
    for s in range(4):
        rows = dot(hot(iota((n, 2048), 1) == known[:, s : s + 1]), memory[...])
        picked[s * n : (s + 1) * n, :] = rows.astype(bf16)
        for c in range(4):
            stage[pl.ds(s * 4 + c, n, stride=16), :] = rows[:, c * 128 : (c + 1) * 128]
    outbox[...] = stage[...].astype(bf16).reshape(n, 16, 128)

    def send_all(source, target, send_sem, recv_sem):
        def send(step, carry):
            peer = (me + step) & (n - 1)
            pltpu.make_async_remote_copy(
                src_ref=source.at[peer],
                dst_ref=target.at[me],
                send_sem=send_sem,
                recv_sem=recv_sem,
                device_id=(peer // groups, peer & (groups - 1)),
                device_id_type=MESH,
            ).start()
            return carry

        lax.fori_loop(1, n, send, 0)

    def all_sent(source, target, send_sem, recv_sem):
        return pltpu.make_async_remote_copy(
            src_ref=source.at[pl.ds(0, n - 1)],
            dst_ref=target.at[pl.ds(0, n - 1)],
            send_sem=send_sem,
            recv_sem=recv_sem,
            device_id=(o, (g + 1) & (groups - 1)),
            device_id_type=MESH,
        )

    own = pltpu.make_async_copy(outbox.at[me], inbox.at[me], own_sem.at[2])
    own.start()
    send_all(outbox, inbox, table_sem.at[0], table_sem.at[1])

    loads[1].wait()
    state[...] = dot(picked[...], w_hidden[...])
    loads[2].wait()
    value_t[...] = w_value[...].astype(f32).T.astype(bf16)
    asked_col = jnp.concatenate([known[:, s : s + 1] for s in range(4)], axis=0)
    count_col = jnp.concatenate([known[:, s + 4 : s + 5] for s in range(4)], axis=0)
    asked_row = jnp.concatenate([known_t[s : s + 1, :] for s in range(4)], axis=1)
    count_row = jnp.concatenate([known_t[s + 4 : s + 5, :] for s in range(4)], axis=1)
    match = asked_col == asked_row
    match_ref[...] = hot(match)
    number = jnp.sum(jnp.where(match, count_row.astype(f32), 0.0), axis=1, keepdims=True)
    share[...] = jnp.broadcast_to(1.0 / jnp.maximum(number, 1.0), share.shape)
    number_row = jnp.sum(jnp.where(match, count_col.astype(f32), 0.0), axis=0, keepdims=True)
    earlier = match & (iota((512, 512), 0) < iota((512, 512), 1))
    earlier = jnp.sum(jnp.where(earlier, 1.0, 0.0), axis=0, keepdims=True)
    leader = jnp.where((earlier == 0.0) & (number_row > 0.0), asked_row, -1)
    leader_out[...] = jnp.broadcast_to(leader, leader_out.shape)
    ev_code[...] = cosine(cols[:, 2:3].astype(f32) * freq_row[...]).astype(bf16)
    src_hot[...] = hot(iota((512, 512), 1) == cols[:, 0:1])
    dst_hot[...] = hot(iota((512, 512), 1) == cols[:, 1:2])
    dst_hot_t[...] = hot(iota((512, 512), 0) == ints[33:34, :])

    own.wait()
    all_sent(outbox, inbox, table_sem.at[0], table_sem.at[1]).wait()
    stage[...] = inbox[...].reshape(n * 16, 128).astype(f32)
    for c in range(4):
        table[:, c * 128 : (c + 1) * 128] = stage[pl.ds(c, 512, stride=4), :].astype(bf16)

    dst_mem = dot(dst_hot[...], table[...])
    src_mem = dot(src_hot[...], table[...]).astype(bf16)
    loads[3].wait()
    loads[4].wait()
    query = dot(dst_mem.astype(bf16), w_query[...]) * (1.0 / 16.0)
    query_hi, query_lo = split(query)
    key_hi, key_lo = split(dot(table[...], w_key[:width, :]))
    for h in range(HEADS):
        part = slice(h * 256, h * 256 + 256)
        full[h] = (
            dot(key_hi[:, part], query_hi[:, part], NT)
            + dot(key_hi[:, part], query_lo[:, part], NT)
            + dot(key_lo[:, part], query_hi[:, part], NT)
        )
        query_code[h] = dot(w_key[width:, part], query_hi[:, part], NT) + dot(
            w_key[width:, part], query_lo[:, part], NT
        )
    val_hi, val_lo = split(dot(value_t[:, :width], table[...], NT))

    def attend(piece, carry):
        lanes = pl.ds(pl.multiple_of(piece * 128, 128), 128)
        near = ints[0:neigh, lanes]
        near8 = [jnp.broadcast_to(near[k : k + 1, :], (8, 128)) for k in range(neigh)]
        sub = iota((8, 128), 0)

        def look(i, sums):
            sums = list(sums)
            for u in range(4):
                base = pl.multiple_of(i * 32 + u * 8, 8)
                place = sub + base
                first = full[0, pl.ds(base, 8), lanes]
                second = full[1, pl.ds(base, 8), lanes]
                for k in range(neigh):
                    mask = place == near8[k]
                    sums[k] = jnp.where(mask, first, sums[k])
                    sums[neigh + k] = jnp.where(mask, second, sums[neigh + k])
            return tuple(sums)

        zero = jnp.zeros((8, 128), f32)
        sums = list(lax.fori_loop(0, 16, look, (zero,) * (2 * neigh)))
        rows = [[], []]
        for h in range(HEADS):
            mine = query_code[h, :, lanes]
            for k in range(neigh):
                prod = (code[k, :, lanes] * mine).reshape(te // 8, 8, 128)
                prod = jnp.sum(prod, axis=0) + sums[h * neigh + k]
                rows[h].append(jnp.sum(prod, axis=0, keepdims=True))
        whole = []
        weights = []
        for h in range(HEADS):
            score = jnp.concatenate(rows[h], axis=0)
            score = jnp.exp(score - jnp.max(score, axis=0, keepdims=True))
            weight = score / jnp.sum(score, axis=0, keepdims=True)
            total = jnp.zeros((neigh, 128), f32)
            for k in range(neigh):
                total += jnp.where(near == near[k : k + 1, :], weight[k : k + 1, :], 0.0)
            weights.append(weight)
            whole.append([jnp.broadcast_to(total[k : k + 1, :], (16, 128)) for k in range(neigh)])
        near16 = [jnp.broadcast_to(near[k : k + 1, :], (16, 128)) for k in range(neigh)]
        sub16 = iota((16, 128), 0)

        def put(i, carry):
            base = pl.multiple_of(i * 16, 16)
            place = sub16 + base
            both = [jnp.zeros((16, 128), f32)] * HEADS
            for k in range(neigh):
                mask = place == near16[k]
                for h in range(HEADS):
                    both[h] = jnp.where(mask, whole[h][k], both[h])
            for h in range(HEADS):
                high, low = split(both[h])
                spread_hi[h, pl.ds(base, 16), lanes] = high
                spread_lo[h, pl.ds(base, 16), lanes] = low
            return carry

        lax.fori_loop(0, 32, put, 0)
        for h in range(HEADS):
            for i in range(te // 16):
                mixed = jnp.zeros((16, 128), f32)
                for k in range(neigh):
                    mixed += code[k, i * 16 : i * 16 + 16, lanes] * weights[h][k : k + 1, :]
                high, low = split(mixed)
                spread_hi[h, width + i * 16 : width + i * 16 + 16, lanes] = high
                spread_lo[h, width + i * 16 : width + i * 16 + 16, lanes] = low
        return carry

    lax.fori_loop(0, 4, attend, 0)
    att = []
    for h in range(HEADS):
        part = slice(h * 256, h * 256 + 256)
        value = jnp.concatenate([val_hi[part], value_t[part, width:]], axis=1)
        att.append(
            dot(value, spread_hi[h])
            + dot(value, spread_lo[h])
            + dot(val_lo[part], spread_hi[h, :width, :])
        )
    att = jnp.concatenate(att, axis=0).T.astype(bf16)
    loads[5].wait()
    emb[...] = (dst_mem + dot(att, w_out[...])).astype(bf16)
    emb_copy = pltpu.make_async_copy(emb, emb_hbm, emb_sem)
    emb_copy.start()
    loads[6].wait()
    hidden = (
        dot(src_mem, w_msg1[:width, :])
        + dot(emb[...], w_msg1[width : 2 * width, :])
        + dot(ev_code[...], w_msg1[2 * width :, :])
    )
    hidden = jnp.maximum(hidden, 0.0).astype(bf16)
    loads[7].wait()
    owns = []
    for half in range(2):
        part = slice(half * 512, half * 512 + 512)
        message = dot(hidden, w_msg2[:, part]).astype(bf16)
        sums = dot(dst_hot_t[...], message)
        for c in range(4):
            stage[pl.ds(c, 512, stride=4), :] = sums[:, c * 128 : (c + 1) * 128]
        part_out[half] = stage[...].astype(bf16).reshape(n, 16, 128)
        own = pltpu.make_async_copy(
            part_out.at[half, me], part_in.at[half, me], own_sem.at[3 + half]
        )
        own.start()
        owns.append(own)
        send_all(
            part_out.at[half], part_in.at[half], part_sem.at[2 * half], part_sem.at[2 * half + 1]
        )
    emb_copy.wait()
    loads[8].wait()
    for half in range(2):
        owns[half].wait()
        all_sent(
            part_out.at[half], part_in.at[half], part_sem.at[2 * half], part_sem.at[2 * half + 1]
        ).wait()
        stage[...] = part_in[half].reshape(n * 16, 128).astype(f32)
        for s in range(4):
            for c in range(4):
                partial[s * n : (s + 1) * n, c * 128 : (c + 1) * 128] = stage[
                    pl.ds(s * 4 + c, n, stride=16), :
                ].astype(bf16)
        total = dot(match_ref[...], partial[...])
        agg = jnp.concatenate(
            [total[:, c * 128 : (c + 1) * 128] * share[...] for c in range(4)], axis=1
        ).astype(bf16)
        gate = dot(agg, w_input[half * 512 : half * 512 + 512, :])
        if half == 0:
            gates[...] = gate
        else:
            gates[...] += gate

    def update_rows(i, carry):
        rows = pl.ds(pl.multiple_of(i * 64, 64), 64)
        reset = jax.nn.sigmoid(gates[rows, 0:width] + state[rows, 0:width])
        update = jax.nn.sigmoid(
            gates[rows, width : 2 * width] + state[rows, width : 2 * width]
        )
        new = jnp.tanh(gates[rows, 2 * width :] + reset * state[rows, 2 * width :])
        old = picked[rows, :].astype(f32)
        fresh_out[rows, :] = ((1.0 - update) * new + update * old).astype(bf16)
        return carry

    lax.fori_loop(0, 8, update_rows, 0)


def place_kernel(leader, fresh, memory, out):
    size = out.shape[0]
    base = pl.program_id(0) * size
    mask = (iota((size, 512), 0) + base) == leader[0:1, :]
    hit = jnp.max(jnp.where(mask, 1.0, 0.0), axis=1, keepdims=True)
    moved = dot(hot(mask), fresh[...])
    out[...] = jnp.where(hit > 0.0, moved, memory[...].astype(f32)).astype(bf16)


def per_device(
    memory,
    touched,
    src_pos,
    dst_owner,
    dst_slot,
    neighbors,
    ev_time,
    neigh_time,
    time_freq,
    w_query,
    w_key,
    w_value,
    w_out,
    w_msg1,
    w_msg2,
    w_input,
    w_hidden,
):
    owner = dst_owner[:, 0]
    dst_pos = owner * 4 + dst_slot
    ints = jnp.concatenate(
        [
            neighbors.T,
            (ev_time[:, None] - neigh_time).T,
            jnp.stack([src_pos, dst_pos, owner, dst_slot, ev_time, ev_time, ev_time, ev_time]),
        ],
        axis=0,
    )
    cols = jnp.stack([src_pos, dst_pos, ev_time], axis=1)
    asks = touched.reshape(16, 8, 4).transpose(1, 0, 2).reshape(128, 4)
    asks = jnp.pad(asks, ((0, 0), (0, 124)))
    vmem = pl.BlockSpec(memory_space=pltpu.VMEM)
    anyw = pl.BlockSpec(memory_space=pl.ANY)
    weights = (w_hidden, w_query, w_key, w_value, w_out, w_msg1, w_msg2, w_input)

    def local(*shape, dtype=bf16):
        return pltpu.VMEM(shape, dtype)

    sems = pltpu.SemaphoreType.DMA
    emb, fresh, leader = pl.pallas_call(
        window_kernel,
        out_shape=(
            jax.ShapeDtypeStruct((512, 512), bf16),
            jax.ShapeDtypeStruct((512, 512), bf16),
            jax.ShapeDtypeStruct((8, 512), i32),
        ),
        in_specs=[vmem] * 5 + [anyw] * 9,
        out_specs=(anyw, vmem, vmem),
        scratch_shapes=[
            local(*memory.shape),
            *[local(*w.shape) for w in weights],
            sems((9,)),
            sems,
            local(128, 128, dtype=i32),
            local(128, 128, dtype=i32),
            local(16, 8, 128, dtype=i32),
            local(16, 8, 128, dtype=i32),
            sems((4,)),
            sems((5,)),
            local(2048, 128, dtype=f32),
            local(128, 16, 128),
            local(128, 16, 128),
            sems((2,)),
            local(2, 128, 16, 128),
            local(2, 128, 16, 128),
            sems((4,)),
            local(16, 128, 512, dtype=f32),
            local(512, 512),
            local(512, 1536, dtype=f32),
            local(512, 640),
            local(512, 512),
            local(512, 128, dtype=f32),
            local(512, 128),
            local(512, 512),
            local(512, 512),
            local(512, 512),
            local(512, 512),
            local(2, 512, 512, dtype=f32),
            local(2, 128, 512, dtype=f32),
            local(2, 640, 512),
            local(2, 640, 512),
            local(512, 512),
            local(512, 512),
            local(512, 1536, dtype=f32),
        ],
        compiler_params=pltpu.CompilerParams(
            collective_id=0, has_side_effects=True, vmem_limit_bytes=60 << 20
        ),
        name="window",
    )(ints, cols, asks, time_freq[:, None], time_freq[None, :], memory, *weights)
    rows = 256
    new_memory = pl.pallas_call(
        place_kernel,
        grid=(memory.shape[0] // rows,),
        out_shape=jax.ShapeDtypeStruct(memory.shape, bf16),
        in_specs=[
            pl.BlockSpec((8, 512), lambda i: (0, 0)),
            pl.BlockSpec((512, 512), lambda i: (0, 0)),
            pl.BlockSpec((rows, 512), lambda i: (i, 0)),
        ],
        out_specs=pl.BlockSpec((rows, 512), lambda i: (i, 0)),
        compiler_params=pltpu.CompilerParams(vmem_limit_bytes=32 << 20),
        name="place",
    )(leader, fresh, memory)
    return emb, new_memory


def solution(mesh):
    rows = P(("owner", "group"))
    in_specs = (rows,) * 8 + (P(),) * 9
    return jax.shard_map(
        per_device, mesh=mesh, in_specs=in_specs, out_specs=(rows, rows), check_vma=False
    )
```

```python
import jax
import jax.numpy as jnp
from jax import lax
from jax.experimental import pallas as pl
from jax.experimental.pallas import tpu as pltpu
from jax.sharding import PartitionSpec as P

HEADS = 2
MESH = pl.DeviceIdType.MESH
f32, bf16, i32 = jnp.float32, jnp.bfloat16, jnp.int32
COS = (
    0.9999992251396179,
    -0.499994158744812,
    0.041659727692604065,
    -0.00138586456887424,
    2.4201255655498244e-05,
    -2.196603787751883e-07,
)
NN = (((1,), (0,)), ((), ()))
NT = (((1,), (1,)), ((), ()))


def dot(a, b, dims=NN):
    return lax.dot_general(a, b, dims, preferred_element_type=f32)


def iota(shape, axis):
    return lax.broadcasted_iota(i32, shape, axis)


def hot(mask):
    return jnp.where(mask, 1.0, 0.0).astype(bf16)


def split(x):
    high = x.astype(bf16)
    return high, (x - high.astype(f32)).astype(bf16)


def cosine(x):
    turns = jnp.floor(x * 0.15915494309189535 + 0.5)
    r = (x - turns * 6.28125) - turns * 0.0019353071795864769
    r = r * r
    y = COS[-1] * r + COS[-2]
    for c in COS[-3::-1]:
        y = y * r + c
    return y


def window_kernel(
    touched,
    src_pos,
    dst_owner,
    dst_slot,
    neighbors,
    ev_time,
    neigh_time,
    time_freq,
    memory_hbm,
    w_hidden_hbm,
    w_query_hbm,
    w_key_hbm,
    w_value_hbm,
    w_out_hbm,
    w_msg1_hbm,
    w_msg2_hbm,
    w_input_hbm,
    emb_hbm,
    new_hbm,
    memory,
    w_hidden,
    w_query,
    w_key,
    w_value,
    w_out,
    w_msg1,
    w_msg2,
    w_input,
    load_sem,
    emb_sem,
    new_sem,
    ints,
    natural,
    note,
    note_in,
    relay,
    notes,
    note_sem,
    own_sem,
    stage,
    outbox,
    inbox,
    table_sem,
    part_out,
    part_in,
    part_sem,
    code,
    picked,
    state,
    value_t,
    match_ref,
    share,
    ev_code,
    src_hot,
    dst_hot,
    dst_hot_t,
    table,
    full,
    query_code,
    spread_hi,
    spread_lo,
    emb,
    partial,
    gates,
    lead,
    taken,
    fresh,
):
    groups, owners = 8, 16
    n = groups * owners
    o, g = lax.axis_index("owner"), lax.axis_index("group")
    me = o * groups + g
    neigh, te, width = 16, 128, 512

    barrier = pltpu.get_barrier_semaphore()
    for step in range(1, groups):
        pl.semaphore_signal(
            barrier, inc=1, device_id=(o, (g + step) & (groups - 1)), device_id_type=MESH
        )
    for step in range(1, owners):
        pl.semaphore_signal(
            barrier, inc=1, device_id=((o + step) & (owners - 1), g), device_id_type=MESH
        )
    loads = []
    for number, (source, target) in enumerate(
        (
            (memory_hbm, memory),
            (w_hidden_hbm, w_hidden),
            (w_value_hbm, w_value),
            (w_query_hbm, w_query),
            (w_key_hbm, w_key),
            (w_out_hbm, w_out),
            (w_msg1_hbm, w_msg1),
            (w_msg2_hbm, w_msg2),
            (w_input_hbm, w_input),
        )
    ):
        load = pltpu.make_async_copy(source, target, load_sem.at[number])
        load.start()
        loads.append(load)

    ints[0:neigh, :] = neighbors[...]
    ints[neigh : 2 * neigh, :] = ev_time[...] - neigh_time[...]
    ints[32:33, :] = src_pos[...]
    ints[33:34, :] = dst_owner[...] * 4 + dst_slot[...]
    ints[34:35, :] = ev_time[...]
    ints[35:40, :] = jnp.zeros((5, 512), i32)
    cols = ints[32:40, :].astype(f32).T.astype(i32)
    freq_row = time_freq[...]
    freq_col = jnp.broadcast_to(freq_row, (8, te)).T[:, 0:1]

    owner_hot = hot(iota((n, 512), 0) == dst_owner[...])
    slot_hot = hot(iota((n, 512), 0) == dst_slot[...] + 4)
    natural[...] = dot(owner_hot, slot_hot, NT).astype(i32)
    wanted = jnp.concatenate([touched[0], touched[0]], axis=0).astype(f32)
    natural[:, 0:4] = wanted.T[:, 0:4].astype(i32)
    for group in range(groups):
        note[group * owners : (group + 1) * owners, :] = natural[
            pl.ds(group, owners, stride=groups), :
        ]
    pl.semaphore_wait(barrier, groups + owners - 2)

    def note_part(index):
        return pl.ds(pl.multiple_of(index * owners, owners), owners)

    own = pltpu.make_async_copy(note.at[note_part(g)], note_in.at[note_part(g)], own_sem.at[0])
    own.start()
    for step in range(1, groups):
        peer = (g + step) & (groups - 1)
        pltpu.make_async_remote_copy(
            src_ref=note.at[note_part(peer)],
            dst_ref=note_in.at[note_part(g)],
            send_sem=note_sem.at[0],
            recv_sem=note_sem.at[1],
            device_id=(o, peer),
            device_id_type=MESH,
        ).start()

    def make_codes(first):
        def codes(k, carry):
            for i in range(te // 32):
                rows = slice(i * 32, i * 32 + 32)
                code[k, rows, :] = cosine(freq_col[rows] * delta).astype(bf16).astype(f32)
            return carry

        for k in range(first, first + neigh // 2):
            delta = ints[k + neigh : k + neigh + 1, :].astype(f32)
            codes(k, 0)

    make_codes(0)
    own.wait()
    some = (groups - 1) * owners
    pltpu.make_async_remote_copy(
        src_ref=note.at[pl.ds(0, some)],
        dst_ref=note_in.at[pl.ds(0, some)],
        send_sem=note_sem.at[0],
        recv_sem=note_sem.at[1],
        device_id=(o, (g + 1) & (groups - 1)),
        device_id_type=MESH,
    ).wait()
    for owner in range(owners):
        relay[owner] = note_in[pl.ds(owner, groups, stride=owners), :]
    own = pltpu.make_async_copy(relay.at[o], notes.at[o], own_sem.at[1])
    own.start()
    for step in range(1, owners):
        peer = (o + step) & (owners - 1)
        pltpu.make_async_remote_copy(
            src_ref=relay.at[peer],
            dst_ref=notes.at[o],
            send_sem=note_sem.at[2],
            recv_sem=note_sem.at[3],
            device_id=(peer, g),
            device_id_type=MESH,
        ).start()
    make_codes(neigh // 2)
    own.wait()
    pltpu.make_async_remote_copy(
        src_ref=relay.at[pl.ds(0, owners - 1)],
        dst_ref=notes.at[pl.ds(0, owners - 1)],
        send_sem=note_sem.at[2],
        recv_sem=note_sem.at[3],
        device_id=((o + 1) & (owners - 1), g),
        device_id_type=MESH,
    ).wait()
    known = notes[...].reshape(n, 128)
    known_t = known.astype(f32).T.astype(i32)

    loads[0].wait()
    for s in range(4):
        rows = dot(hot(iota((n, 2048), 1) == known[:, s : s + 1]), memory[...])
        picked[s * n : (s + 1) * n, :] = rows.astype(bf16)
        for c in range(4):
            stage[pl.ds(s * 4 + c, n, stride=16), :] = rows[:, c * 128 : (c + 1) * 128]
    outbox[...] = stage[...].astype(bf16).reshape(n, 16, 128)

    def send_all(source, target, send_sem, recv_sem):
        def send(step, carry):
            peer = (me + step) & (n - 1)
            pltpu.make_async_remote_copy(
                src_ref=source.at[peer],
                dst_ref=target.at[me],
                send_sem=send_sem,
                recv_sem=recv_sem,
                device_id=(peer // groups, peer & (groups - 1)),
                device_id_type=MESH,
            ).start()
            return carry

        lax.fori_loop(1, n, send, 0)

    def all_sent(source, target, send_sem, recv_sem):
        return pltpu.make_async_remote_copy(
            src_ref=source.at[pl.ds(0, n - 1)],
            dst_ref=target.at[pl.ds(0, n - 1)],
            send_sem=send_sem,
            recv_sem=recv_sem,
            device_id=(o, (g + 1) & (groups - 1)),
            device_id_type=MESH,
        )

    own = pltpu.make_async_copy(outbox.at[me], inbox.at[me], own_sem.at[2])
    own.start()
    send_all(outbox, inbox, table_sem.at[0], table_sem.at[1])

    loads[1].wait()
    state[...] = dot(picked[...], w_hidden[...])
    loads[2].wait()
    value_t[...] = w_value[...].astype(f32).T.astype(bf16)
    asked_col = jnp.concatenate([known[:, s : s + 1] for s in range(4)], axis=0)
    count_col = jnp.concatenate([known[:, s + 4 : s + 5] for s in range(4)], axis=0)
    asked_row = jnp.concatenate([known_t[s : s + 1, :] for s in range(4)], axis=1)
    count_row = jnp.concatenate([known_t[s + 4 : s + 5, :] for s in range(4)], axis=1)
    match = asked_col == asked_row
    match_ref[...] = hot(match)
    number = jnp.sum(jnp.where(match, count_row.astype(f32), 0.0), axis=1, keepdims=True)
    share[...] = jnp.broadcast_to(1.0 / jnp.maximum(number, 1.0), share.shape)
    number_row = jnp.sum(jnp.where(match, count_col.astype(f32), 0.0), axis=0, keepdims=True)
    earlier = match & (iota((512, 512), 0) < iota((512, 512), 1))
    earlier = jnp.sum(jnp.where(earlier, 1.0, 0.0), axis=0, keepdims=True)
    leader = jnp.where((earlier == 0.0) & (number_row > 0.0), asked_row, -1)
    for i in range(8):
        rows = slice(i * 256, i * 256 + 256)
        mask = (iota((256, 512), 0) + i * 256) == leader
        lead[rows, :] = hot(mask)
        hit = jnp.max(jnp.where(mask, 1.0, 0.0), axis=1, keepdims=True)
        taken[rows, :] = jnp.broadcast_to(hit, (256, 128))
    ev_code[...] = cosine(cols[:, 2:3].astype(f32) * freq_row).astype(bf16)
    src_hot[...] = hot(iota((512, 512), 1) == cols[:, 0:1])
    dst_hot[...] = hot(iota((512, 512), 1) == cols[:, 1:2])
    dst_hot_t[...] = hot(iota((512, 512), 0) == ints[33:34, :])

    own.wait()
    all_sent(outbox, inbox, table_sem.at[0], table_sem.at[1]).wait()
    stage[...] = inbox[...].reshape(n * 16, 128).astype(f32)
    for c in range(4):
        table[:, c * 128 : (c + 1) * 128] = stage[pl.ds(c, 512, stride=4), :].astype(bf16)

    dst_mem = dot(dst_hot[...], table[...])
    src_mem = dot(src_hot[...], table[...]).astype(bf16)
    loads[3].wait()
    loads[4].wait()
    query = dot(dst_mem.astype(bf16), w_query[...]) * (1.0 / 16.0)
    query_hi, query_lo = split(query)
    key_hi, key_lo = split(dot(table[...], w_key[:width, :]))
    for h in range(HEADS):
        part = slice(h * 256, h * 256 + 256)
        full[h] = (
            dot(key_hi[:, part], query_hi[:, part], NT)
            + dot(key_hi[:, part], query_lo[:, part], NT)
            + dot(key_lo[:, part], query_hi[:, part], NT)
        )
        query_code[h] = dot(w_key[width:, part], query_hi[:, part], NT) + dot(
            w_key[width:, part], query_lo[:, part], NT
        )
    val_hi, val_lo = split(dot(value_t[:, :width], table[...], NT))

    def attend(piece, carry):
        lanes = pl.ds(pl.multiple_of(piece * 128, 128), 128)
        near = ints[0:neigh, lanes]
        near8 = [jnp.broadcast_to(near[k : k + 1, :], (8, 128)) for k in range(neigh)]
        sub = iota((8, 128), 0)

        def look(i, sums):
            sums = list(sums)
            for u in range(4):
                base = pl.multiple_of(i * 32 + u * 8, 8)
                place = sub + base
                first = full[0, pl.ds(base, 8), lanes]
                second = full[1, pl.ds(base, 8), lanes]
                for k in range(neigh):
                    mask = place == near8[k]
                    sums[k] = jnp.where(mask, first, sums[k])
                    sums[neigh + k] = jnp.where(mask, second, sums[neigh + k])
            return tuple(sums)

        zero = jnp.zeros((8, 128), f32)
        sums = list(lax.fori_loop(0, 16, look, (zero,) * (2 * neigh)))
        rows = [[], []]
        for h in range(HEADS):
            mine = query_code[h, :, lanes]
            for k in range(neigh):
                prod = (code[k, :, lanes] * mine).reshape(te // 8, 8, 128)
                prod = jnp.sum(prod, axis=0) + sums[h * neigh + k]
                rows[h].append(jnp.sum(prod, axis=0, keepdims=True))
        whole = []
        weights = []
        for h in range(HEADS):
            score = jnp.concatenate(rows[h], axis=0)
            score = jnp.exp(score - jnp.max(score, axis=0, keepdims=True))
            weight = score / jnp.sum(score, axis=0, keepdims=True)
            total = jnp.zeros((neigh, 128), f32)
            for k in range(neigh):
                total += jnp.where(near == near[k : k + 1, :], weight[k : k + 1, :], 0.0)
            weights.append(weight)
            whole.append([jnp.broadcast_to(total[k : k + 1, :], (16, 128)) for k in range(neigh)])
        near16 = [jnp.broadcast_to(near[k : k + 1, :], (16, 128)) for k in range(neigh)]
        sub16 = iota((16, 128), 0)

        def put(i, carry):
            base = pl.multiple_of(i * 16, 16)
            place = sub16 + base
            both = [jnp.zeros((16, 128), f32)] * HEADS
            for k in range(neigh):
                mask = place == near16[k]
                for h in range(HEADS):
                    both[h] = jnp.where(mask, whole[h][k], both[h])
            for h in range(HEADS):
                high, low = split(both[h])
                spread_hi[h, pl.ds(base, 16), lanes] = high
                spread_lo[h, pl.ds(base, 16), lanes] = low
            return carry

        lax.fori_loop(0, 32, put, 0)
        for h in range(HEADS):
            for i in range(te // 16):
                mixed = jnp.zeros((16, 128), f32)
                for k in range(neigh):
                    mixed += code[k, i * 16 : i * 16 + 16, lanes] * weights[h][k : k + 1, :]
                high, low = split(mixed)
                spread_hi[h, width + i * 16 : width + i * 16 + 16, lanes] = high
                spread_lo[h, width + i * 16 : width + i * 16 + 16, lanes] = low
        return carry

    lax.fori_loop(0, 4, attend, 0)
    att = []
    for h in range(HEADS):
        part = slice(h * 256, h * 256 + 256)
        value = jnp.concatenate([val_hi[part], value_t[part, width:]], axis=1)
        att.append(
            dot(value, spread_hi[h])
            + dot(value, spread_lo[h])
            + dot(val_lo[part], spread_hi[h, :width, :])
        )
    att = jnp.concatenate(att, axis=0).T.astype(bf16)
    loads[5].wait()
    emb[...] = (dst_mem + dot(att, w_out[...])).astype(bf16)
    emb_copy = pltpu.make_async_copy(emb, emb_hbm, emb_sem)
    emb_copy.start()
    loads[6].wait()
    hidden = (
        dot(src_mem, w_msg1[:width, :])
        + dot(emb[...], w_msg1[width : 2 * width, :])
        + dot(ev_code[...], w_msg1[2 * width :, :])
    )
    hidden = jnp.maximum(hidden, 0.0).astype(bf16)
    loads[7].wait()
    owns = []
    for half in range(2):
        part = slice(half * 512, half * 512 + 512)
        message = dot(hidden, w_msg2[:, part]).astype(bf16)
        sums = dot(dst_hot_t[...], message)
        for c in range(4):
            stage[pl.ds(c, 512, stride=4), :] = sums[:, c * 128 : (c + 1) * 128]
        part_out[half] = stage[...].astype(bf16).reshape(n, 16, 128)
        own = pltpu.make_async_copy(
            part_out.at[half, me], part_in.at[half, me], own_sem.at[3 + half]
        )
        own.start()
        owns.append(own)
        send_all(
            part_out.at[half], part_in.at[half], part_sem.at[2 * half], part_sem.at[2 * half + 1]
        )
    emb_copy.wait()
    loads[8].wait()
    for half in range(2):
        owns[half].wait()
        all_sent(
            part_out.at[half], part_in.at[half], part_sem.at[2 * half], part_sem.at[2 * half + 1]
        ).wait()
        stage[...] = part_in[half].reshape(n * 16, 128).astype(f32)
        for s in range(4):
            for c in range(4):
                partial[s * n : (s + 1) * n, c * 128 : (c + 1) * 128] = stage[
                    pl.ds(s * 4 + c, n, stride=16), :
                ].astype(bf16)
        total = dot(match_ref[...], partial[...])
        agg = jnp.concatenate(
            [total[:, c * 128 : (c + 1) * 128] * share[...] for c in range(4)], axis=1
        ).astype(bf16)
        gate = dot(agg, w_input[half * 512 : half * 512 + 512, :])
        if half == 0:
            gates[...] = gate
        else:
            gates[...] += gate

    def update_rows(i, carry):
        rows = pl.ds(pl.multiple_of(i * 64, 64), 64)
        reset = jax.nn.sigmoid(gates[rows, 0:width] + state[rows, 0:width])
        update = jax.nn.sigmoid(
            gates[rows, width : 2 * width] + state[rows, width : 2 * width]
        )
        new = jnp.tanh(gates[rows, 2 * width :] + reset * state[rows, 2 * width :])
        old = picked[rows, :].astype(f32)
        fresh[rows, :] = ((1.0 - update) * new + update * old).astype(bf16)
        return carry

    lax.fori_loop(0, 8, update_rows, 0)

    def place(i, carry):
        rows = pl.ds(pl.multiple_of(i * 256, 256), 256)
        moved = dot(lead[rows, :], fresh[...])
        mask = taken[rows, :] > 0.0
        for c in range(4):
            lanes = slice(c * 128, c * 128 + 128)
            old = memory[rows, lanes].astype(f32)
            memory[rows, lanes] = jnp.where(mask, moved[:, lanes], old).astype(bf16)
        pltpu.make_async_copy(memory.at[rows], new_hbm.at[rows], new_sem).start()
        return carry

    lax.fori_loop(0, 8, place, 0)
    pltpu.make_async_copy(memory, new_hbm, new_sem).wait()


def per_device(
    memory,
    touched,
    src_pos,
    dst_owner,
    dst_slot,
    neighbors,
    ev_time,
    neigh_time,
    time_freq,
    w_query,
    w_key,
    w_value,
    w_out,
    w_msg1,
    w_msg2,
    w_input,
    w_hidden,
):
    vmem = pl.BlockSpec(memory_space=pltpu.VMEM)
    anyw = pl.BlockSpec(memory_space=pl.ANY)
    weights = (w_hidden, w_query, w_key, w_value, w_out, w_msg1, w_msg2, w_input)

    def local(*shape, dtype=bf16):
        return pltpu.VMEM(shape, dtype)

    sems = pltpu.SemaphoreType.DMA
    return pl.pallas_call(
        window_kernel,
        out_shape=(
            jax.ShapeDtypeStruct((512, 512), bf16),
            jax.ShapeDtypeStruct(memory.shape, bf16),
        ),
        in_specs=[vmem] * 8 + [anyw] * 9,
        out_specs=(anyw, anyw),
        scratch_shapes=[
            local(*memory.shape),
            *[local(*w.shape) for w in weights],
            sems((9,)),
            sems,
            sems,
            local(40, 512, dtype=i32),
            local(128, 128, dtype=i32),
            local(128, 128, dtype=i32),
            local(128, 128, dtype=i32),
            local(16, 8, 128, dtype=i32),
            local(16, 8, 128, dtype=i32),
            sems((4,)),
            sems((5,)),
            local(2048, 128, dtype=f32),
            local(128, 16, 128),
            local(128, 16, 128),
            sems((2,)),
            local(2, 128, 16, 128),
            local(2, 128, 16, 128),
            sems((4,)),
            local(16, 128, 512, dtype=f32),
            local(512, 512),
            local(512, 1536, dtype=f32),
            local(512, 640),
            local(512, 512),
            local(512, 128, dtype=f32),
            local(512, 128),
            local(512, 512),
            local(512, 512),
            local(512, 512),
            local(512, 512),
            local(2, 512, 512, dtype=f32),
            local(2, 128, 512, dtype=f32),
            local(2, 640, 512),
            local(2, 640, 512),
            local(512, 512),
            local(512, 512),
            local(512, 1536, dtype=f32),
            local(*memory.shape),
            local(memory.shape[0], 128, dtype=f32),
            local(512, 512),
        ],
        compiler_params=pltpu.CompilerParams(
            collective_id=0, has_side_effects=True, vmem_limit_bytes=60 << 20
        ),
        name="window",
    )(
        touched.transpose(0, 2, 1),
        src_pos[None, :],
        dst_owner.reshape(1, -1),
        dst_slot[None, :],
        neighbors.T,
        ev_time[None, :],
        neigh_time.T,
        time_freq[None, :],
        memory,
        *weights,
    )


def solution(mesh):
    rows = P(("owner", "group"))
    in_specs = (rows,) * 8 + (P(),) * 9
    return jax.shard_map(
        per_device, mesh=mesh, in_specs=in_specs, out_specs=(rows, rows), check_vma=False
    )
```

```python
import jax
import jax.numpy as jnp
from jax import lax
from jax.experimental import pallas as pl
from jax.experimental.pallas import tpu as pltpu
from jax.sharding import PartitionSpec as P

HEADS = 2
MESH = pl.DeviceIdType.MESH
f32, bf16, i32 = jnp.float32, jnp.bfloat16, jnp.int32
COS = (
    0.9999992251396179,
    -0.499994158744812,
    0.041659727692604065,
    -0.00138586456887424,
    2.4201255655498244e-05,
    -2.196603787751883e-07,
)
NN = (((1,), (0,)), ((), ()))
NT = (((1,), (1,)), ((), ()))


def dot(a, b, dims=NN):
    return lax.dot_general(a, b, dims, preferred_element_type=f32)


def iota(shape, axis):
    return lax.broadcasted_iota(i32, shape, axis)


def hot(mask):
    return jnp.where(mask, 1.0, 0.0).astype(bf16)


def split(x):
    high = x.astype(bf16)
    return high, (x - high.astype(f32)).astype(bf16)


def take(x, index):
    return jnp.take_along_axis(x, index, axis=0, mode="promise_in_bounds")


def cosine(x):
    turns = jnp.floor(x * 0.15915494309189535 + 0.5)
    r = (x - turns * 6.28125) - turns * 0.0019353071795864769
    r = r * r
    y = COS[-1] * r + COS[-2]
    for c in COS[-3::-1]:
        y = y * r + c
    return y


def window_kernel(
    touched,
    src_pos,
    dst_owner,
    dst_slot,
    neighbors,
    ev_time,
    neigh_time,
    time_freq,
    memory_hbm,
    w_hidden_hbm,
    w_query_hbm,
    w_key_hbm,
    w_value_hbm,
    w_out_hbm,
    w_msg1_hbm,
    w_msg2_hbm,
    w_input_hbm,
    emb_hbm,
    fresh_hbm,
    lead_hbm,
    memory,
    w_hidden,
    w_query,
    w_key,
    w_value,
    w_out,
    w_msg1,
    w_msg2,
    w_input,
    load_sem,
    emb_sem,
    new_sem,
    ints,
    natural,
    note,
    notes,
    note_sem,
    own_sem,
    stage,
    outbox,
    inbox,
    table_sem,
    part_out,
    part_in,
    part_sem,
    code,
    picked,
    state,
    value_t,
    match_ref,
    share,
    ev_code,
    src_hot,
    dst_hot,
    dst_hot_t,
    table,
    full,
    query_code,
    spread_hi,
    spread_lo,
    emb,
    partial,
    gates,
    lead,
    lead_sem,
    fresh,
    finder,
):
    groups, owners = 8, 16
    n = groups * owners
    o, g = lax.axis_index("owner"), lax.axis_index("group")
    me = o * groups + g
    neigh, te, width = 16, 128, 512

    barrier = pltpu.get_barrier_semaphore()

    def greet(step, carry):
        peer = (me + step) & (n - 1)
        pl.semaphore_signal(
            barrier,
            inc=1,
            device_id=(peer // groups, peer & (groups - 1)),
            device_id_type=MESH,
        )
        return carry

    lax.fori_loop(1, n, greet, 0)
    loads = []
    for number, (source, target) in enumerate(
        (
            (memory_hbm, memory),
            (w_hidden_hbm, w_hidden),
            (w_value_hbm, w_value),
            (w_query_hbm, w_query),
            (w_key_hbm, w_key),
            (w_out_hbm, w_out),
            (w_msg1_hbm, w_msg1),
            (w_msg2_hbm, w_msg2),
            (w_input_hbm, w_input),
        )
    ):
        load = pltpu.make_async_copy(source, target, load_sem.at[number])
        load.start()
        loads.append(load)

    ints[0:neigh, :] = neighbors[...]
    ints[neigh : 2 * neigh, :] = ev_time[...] - neigh_time[...]
    ints[32:33, :] = src_pos[...]
    ints[33:34, :] = dst_owner[...] * 4 + dst_slot[...]
    ints[34:35, :] = ev_time[...]
    ints[35:40, :] = jnp.zeros((5, 512), i32)
    cols = ints[32:40, :].astype(f32).T.astype(i32)
    freq_row = time_freq[...]
    freq_col = jnp.broadcast_to(freq_row, (8, te)).T[:, 0:1]

    owner_hot = hot(iota((n, 512), 0) == dst_owner[...])
    slot_hot = hot(iota((n, 512), 0) == dst_slot[...] + 4)
    natural[...] = dot(owner_hot, slot_hot, NT).astype(i32)
    wanted = jnp.concatenate([touched[0], touched[0]], axis=0).astype(f32)
    natural[:, 0:4] = wanted.T[:, 0:4].astype(i32)
    note[:, 0, :] = natural[...]
    pl.semaphore_wait(barrier, n - 1)

    def send_all(source, target, send_sem, recv_sem):
        def send(step, carry):
            peer = (me + step) & (n - 1)
            pltpu.make_async_remote_copy(
                src_ref=source.at[peer],
                dst_ref=target.at[me],
                send_sem=send_sem,
                recv_sem=recv_sem,
                device_id=(peer // groups, peer & (groups - 1)),
                device_id_type=MESH,
            ).start()
            return carry

        lax.fori_loop(1, n, send, 0)

    def all_sent(source, target, send_sem, recv_sem):
        return pltpu.make_async_remote_copy(
            src_ref=source.at[pl.ds(0, n - 1)],
            dst_ref=target.at[pl.ds(0, n - 1)],
            send_sem=send_sem,
            recv_sem=recv_sem,
            device_id=(o, (g + 1) & (groups - 1)),
            device_id_type=MESH,
        )

    own = pltpu.make_async_copy(note.at[me], notes.at[me], own_sem.at[0])
    own.start()
    send_all(note, notes, note_sem.at[0], note_sem.at[1])

    def make_codes(first):
        def codes(k, carry):
            for i in range(te // 32):
                rows = slice(i * 32, i * 32 + 32)
                code[k, rows, :] = cosine(freq_col[rows] * delta).astype(bf16).astype(f32)
            return carry

        for k in range(first, first + neigh // 2):
            delta = ints[k + neigh : k + neigh + 1, :].astype(f32)
            codes(k, 0)

    make_codes(0)
    make_codes(neigh // 2)

    def find(piece, carry):
        lanes = pl.ds(pl.multiple_of(piece * 128, 128), 128)
        near = ints[0:neigh, lanes]
        near8 = [jnp.broadcast_to(near[k : k + 1, :], (8, 128)) for k in range(neigh)]
        sub = iota((8, 128), 0)

        def scan(i, carry):
            for u in range(4):
                base = pl.multiple_of(i * 32 + u * 8, 8)
                which = jnp.full((8, 128), neigh, i32)
                for k in range(neigh):
                    which = jnp.where(sub + base == near8[k], k, which)
                finder[pl.ds(base, 8), lanes] = which
            return carry

        lax.fori_loop(0, 16, scan, 0)
        return carry

    lax.fori_loop(0, 4, find, 0)
    own.wait()
    all_sent(note, notes, note_sem.at[0], note_sem.at[1]).wait()
    known = notes[:, 0, :]
    known_t = known.astype(f32).T.astype(i32)

    loads[0].wait()
    for s in range(4):
        rows = dot(hot(iota((n, 2048), 1) == known[:, s : s + 1]), memory[...])
        picked[s * n : (s + 1) * n, :] = rows.astype(bf16)
        for c in range(4):
            stage[pl.ds(s * 4 + c, n, stride=16), :] = rows[:, c * 128 : (c + 1) * 128]
    outbox[...] = stage[...].astype(bf16).reshape(n, 16, 128)

    own = pltpu.make_async_copy(outbox.at[me], inbox.at[me], own_sem.at[2])
    own.start()
    send_all(outbox, inbox, table_sem.at[0], table_sem.at[1])

    loads[1].wait()
    state[...] = dot(picked[...], w_hidden[...])
    loads[2].wait()
    value_t[...] = w_value[...].astype(f32).T.astype(bf16)
    asked_col = jnp.concatenate([known[:, s : s + 1] for s in range(4)], axis=0)
    count_col = jnp.concatenate([known[:, s + 4 : s + 5] for s in range(4)], axis=0)
    asked_row = jnp.concatenate([known_t[s : s + 1, :] for s in range(4)], axis=1)
    count_row = jnp.concatenate([known_t[s + 4 : s + 5, :] for s in range(4)], axis=1)
    match = asked_col == asked_row
    match_ref[...] = hot(match)
    number = jnp.sum(jnp.where(match, count_row.astype(f32), 0.0), axis=1, keepdims=True)
    share[...] = jnp.broadcast_to(1.0 / jnp.maximum(number, 1.0), share.shape)
    number_row = jnp.sum(jnp.where(match, count_col.astype(f32), 0.0), axis=0, keepdims=True)
    earlier = match & (iota((512, 512), 0) < iota((512, 512), 1))
    earlier = jnp.sum(jnp.where(earlier, 1.0, 0.0), axis=0, keepdims=True)
    leader = jnp.where((earlier == 0.0) & (number_row > 0.0), asked_row, -1)
    lead[...] = jnp.broadcast_to(leader, lead.shape)
    lead_copy = pltpu.make_async_copy(lead, lead_hbm, lead_sem)
    lead_copy.start()
    ev_code[...] = cosine(cols[:, 2:3].astype(f32) * freq_row).astype(bf16)
    src_hot[...] = hot(iota((512, 512), 1) == cols[:, 0:1])
    dst_hot[...] = hot(iota((512, 512), 1) == cols[:, 1:2])
    dst_hot_t[...] = hot(iota((512, 512), 0) == ints[33:34, :])

    own.wait()
    all_sent(outbox, inbox, table_sem.at[0], table_sem.at[1]).wait()
    stage[...] = inbox[...].reshape(n * 16, 128).astype(f32)
    for c in range(4):
        table[:, c * 128 : (c + 1) * 128] = stage[pl.ds(c, 512, stride=4), :].astype(bf16)

    dst_mem = dot(dst_hot[...], table[...])
    src_mem = dot(src_hot[...], table[...]).astype(bf16)
    loads[3].wait()
    loads[4].wait()
    query = dot(dst_mem.astype(bf16), w_query[...]) * (1.0 / 16.0)
    query_hi, query_lo = split(query)
    key_hi, key_lo = split(dot(table[...], w_key[:width, :]))
    for h in range(HEADS):
        part = slice(h * 256, h * 256 + 256)
        full[h] = (
            dot(key_hi[:, part], query_hi[:, part], NT)
            + dot(key_hi[:, part], query_lo[:, part], NT)
            + dot(key_lo[:, part], query_hi[:, part], NT)
        )
        query_code[h] = dot(w_key[width:, part], query_hi[:, part], NT) + dot(
            w_key[width:, part], query_lo[:, part], NT
        )
    val_hi, val_lo = split(dot(value_t[:, :width], table[...], NT))

    def attend(piece, carry):
        lanes = pl.ds(pl.multiple_of(piece * 128, 128), 128)
        near = ints[0:neigh, lanes]
        fine = [near[b * 8 : b * 8 + 8, :] & 7 for b in range(2)]
        coarse = [near[b * 8 : b * 8 + 8, :] >> 3 for b in range(2)]

        def look(i, found):
            found = list(found)
            for u in range(8):
                base = pl.multiple_of(i * 64 + u * 8, 8)
                for b in range(2):
                    mask = coarse[b] == i * 8 + u
                    for h in range(HEADS):
                        taken = take(full[h, pl.ds(base, 8), lanes], fine[b])
                        found[h * 2 + b] = jnp.where(mask, taken, found[h * 2 + b])
            return tuple(found)

        zero = jnp.zeros((8, 128), f32)
        found = lax.fori_loop(0, 8, look, (zero,) * (2 * HEADS))

        def timed(i, sums):
            sums = list(sums)
            rows = pl.ds(pl.multiple_of(i * 8, 8), 8)
            mine = [query_code[h, rows, lanes] for h in range(HEADS)]
            for k in range(neigh):
                one = code[k, rows, lanes]
                for h in range(HEADS):
                    sums[h * neigh + k] += one * mine[h]
            return tuple(sums)

        sums = lax.fori_loop(0, te // 8, timed, (zero,) * (HEADS * neigh))
        whole = []
        weights = []
        for h in range(HEADS):
            score = jnp.concatenate(
                [
                    jnp.sum(sums[h * neigh + k], axis=0, keepdims=True)
                    for k in range(neigh)
                ],
                axis=0,
            ) + jnp.concatenate(found[h * 2 : h * 2 + 2], axis=0)
            score = jnp.exp(score - jnp.max(score, axis=0, keepdims=True))
            weight = score / jnp.sum(score, axis=0, keepdims=True)
            total = jnp.zeros((neigh, 128), f32)
            for k in range(neigh):
                total += jnp.where(near == near[k : k + 1, :], weight[k : k + 1, :], 0.0)
            weights.append(weight)
            whole.append([total[0:8, :], total[8:16, :]])

        def put(i, carry):
            for u in range(4):
                base = pl.multiple_of(i * 64 + u * 16, 16)
                both = [[], []]
                for v in range(2):
                    which = finder[pl.ds(base + v * 8, 8), lanes]
                    fine = which & 7
                    for h in range(HEADS):
                        first = jnp.where(which < 8, take(whole[h][0], fine), 0.0)
                        second = take(whole[h][1], fine)
                        both[h].append(
                            jnp.where((which & 24) == 8, second, first)
                        )
                for h in range(HEADS):
                    high, low = split(jnp.concatenate(both[h], axis=0))
                    spread_hi[h, pl.ds(base, 16), lanes] = high
                    spread_lo[h, pl.ds(base, 16), lanes] = low
            return carry

        lax.fori_loop(0, 8, put, 0)
        spread = [
            [jnp.broadcast_to(weights[h][k : k + 1, :], (8, 128)) for k in range(neigh)]
            for h in range(HEADS)
        ]

        def mix(i, carry):
            base = pl.multiple_of(i * 16, 16)
            both = [[], []]
            for v in range(2):
                mixed = [zero] * HEADS
                for k in range(neigh):
                    one = code[k, pl.ds(base + v * 8, 8), lanes]
                    for h in range(HEADS):
                        mixed[h] += one * spread[h][k]
                for h in range(HEADS):
                    both[h].append(mixed[h])
            for h in range(HEADS):
                high, low = split(jnp.concatenate(both[h], axis=0))
                spread_hi[h, pl.ds(width + base, 16), lanes] = high
                spread_lo[h, pl.ds(width + base, 16), lanes] = low
            return carry

        lax.fori_loop(0, te // 16, mix, 0)
        return carry

    lax.fori_loop(0, 4, attend, 0)
    att = []
    for h in range(HEADS):
        part = slice(h * 256, h * 256 + 256)
        value = jnp.concatenate([val_hi[part], value_t[part, width:]], axis=1)
        att.append(
            dot(value, spread_hi[h])
            + dot(value, spread_lo[h])
            + dot(val_lo[part], spread_hi[h, :width, :])
        )
    att = jnp.concatenate(att, axis=0).T.astype(bf16)
    loads[5].wait()
    emb[...] = (dst_mem + dot(att, w_out[...])).astype(bf16)
    emb_copy = pltpu.make_async_copy(emb, emb_hbm, emb_sem)
    emb_copy.start()
    loads[6].wait()
    hidden = (
        dot(src_mem, w_msg1[:width, :])
        + dot(emb[...], w_msg1[width : 2 * width, :])
        + dot(ev_code[...], w_msg1[2 * width :, :])
    )
    hidden = jnp.maximum(hidden, 0.0).astype(bf16)
    loads[7].wait()
    owns = []
    for half in range(2):
        part = slice(half * 512, half * 512 + 512)
        message = dot(hidden, w_msg2[:, part]).astype(bf16)
        sums = dot(dst_hot_t[...], message)
        for c in range(4):
            stage[pl.ds(c, 512, stride=4), :] = sums[:, c * 128 : (c + 1) * 128]
        part_out[half] = stage[...].astype(bf16).reshape(n, 16, 128)
        own = pltpu.make_async_copy(
            part_out.at[half, me], part_in.at[half, me], own_sem.at[3 + half]
        )
        own.start()
        owns.append(own)
        send_all(
            part_out.at[half], part_in.at[half], part_sem.at[2 * half], part_sem.at[2 * half + 1]
        )
    emb_copy.wait()
    loads[8].wait()
    for half in range(2):
        owns[half].wait()
        all_sent(
            part_out.at[half], part_in.at[half], part_sem.at[2 * half], part_sem.at[2 * half + 1]
        ).wait()
        stage[...] = part_in[half].reshape(n * 16, 128).astype(f32)
        for s in range(4):
            for c in range(4):
                partial[s * n : (s + 1) * n, c * 128 : (c + 1) * 128] = stage[
                    pl.ds(s * 4 + c, n, stride=16), :
                ].astype(bf16)
        total = dot(match_ref[...], partial[...])
        agg = jnp.concatenate(
            [total[:, c * 128 : (c + 1) * 128] * share[...] for c in range(4)], axis=1
        ).astype(bf16)
        gate = dot(agg, w_input[half * 512 : half * 512 + 512, :])
        if half == 0:
            gates[...] = gate
        else:
            gates[...] += gate

    def update_rows(i, carry):
        rows = pl.ds(pl.multiple_of(i * 64, 64), 64)
        reset = jax.nn.sigmoid(gates[rows, 0:width] + state[rows, 0:width])
        update = jax.nn.sigmoid(
            gates[rows, width : 2 * width] + state[rows, width : 2 * width]
        )
        new = jnp.tanh(gates[rows, 2 * width :] + reset * state[rows, 2 * width :])
        old = picked[rows, :].astype(f32)
        fresh[rows, :] = ((1.0 - update) * new + update * old).astype(bf16)
        return carry

    lax.fori_loop(0, 8, update_rows, 0)

    fresh_copy = pltpu.make_async_copy(fresh, fresh_hbm, new_sem)
    fresh_copy.start()
    lead_copy.wait()
    fresh_copy.wait()


def place_kernel(
    leader_hbm,
    fresh_hbm,
    memory_hbm,
    emb_hbm,
    emb_out,
    new_hbm,
    leader,
    fresh,
    memory,
    moved,
    sem,
    in_sem,
    out_sem,
):
    emb_copy = pltpu.make_async_copy(emb_hbm, emb_out, sem.at[0])
    emb_copy.start()
    leader_copy = pltpu.make_async_copy(leader_hbm, leader, sem.at[1])
    leader_copy.start()
    fresh_copy = pltpu.make_async_copy(fresh_hbm, fresh, sem.at[2])
    fresh_copy.start()
    blocks = []
    for i in range(8):
        rows = pl.ds(i * 256, 256)
        block = pltpu.make_async_copy(memory_hbm.at[rows], memory.at[rows], in_sem.at[i])
        block.start()
        blocks.append(block)
    leader_copy.wait()
    outs = []
    for i in range(8):
        rows = slice(i * 256, i * 256 + 256)
        mask = iota((256, 512), 0) + i * 256 == leader[0:1, :]
        hit = jnp.max(jnp.where(mask, 1.0, 0.0), axis=1, keepdims=True)
        if i == 0:
            fresh_copy.wait()
        new = dot(hot(mask), fresh[...])
        blocks[i].wait()
        moved[rows, :] = jnp.where(hit > 0.0, new, memory[rows, :].astype(f32)).astype(bf16)
        rows = pl.ds(i * 256, 256)
        out = pltpu.make_async_copy(moved.at[rows], new_hbm.at[rows], out_sem.at[i])
        out.start()
        outs.append(out)
    emb_copy.wait()
    for out in outs:
        out.wait()


def per_device(
    memory,
    touched,
    src_pos,
    dst_owner,
    dst_slot,
    neighbors,
    ev_time,
    neigh_time,
    time_freq,
    w_query,
    w_key,
    w_value,
    w_out,
    w_msg1,
    w_msg2,
    w_input,
    w_hidden,
):
    vmem = pl.BlockSpec(memory_space=pltpu.VMEM)
    anyw = pl.BlockSpec(memory_space=pl.ANY)
    weights = (w_hidden, w_query, w_key, w_value, w_out, w_msg1, w_msg2, w_input)

    def local(*shape, dtype=bf16):
        return pltpu.VMEM(shape, dtype)

    sems = pltpu.SemaphoreType.DMA
    emb, fresh, leader = pl.pallas_call(
        window_kernel,
        out_shape=(
            jax.ShapeDtypeStruct((512, 512), bf16),
            jax.ShapeDtypeStruct((512, 512), bf16),
            jax.ShapeDtypeStruct((8, 512), i32),
        ),
        in_specs=[vmem] * 8 + [anyw] * 9,
        out_specs=(anyw,) * 3,
        scratch_shapes=[
            local(*memory.shape),
            *[local(*w.shape) for w in weights],
            sems((9,)),
            sems,
            sems,
            local(40, 512, dtype=i32),
            local(128, 128, dtype=i32),
            local(128, 1, 128, dtype=i32),
            local(128, 1, 128, dtype=i32),
            sems((2,)),
            sems((5,)),
            local(2048, 128, dtype=f32),
            local(128, 16, 128),
            local(128, 16, 128),
            sems((2,)),
            local(2, 128, 16, 128),
            local(2, 128, 16, 128),
            sems((4,)),
            local(16, 128, 512, dtype=f32),
            local(512, 512),
            local(512, 1536, dtype=f32),
            local(512, 640),
            local(512, 512),
            local(512, 128, dtype=f32),
            local(512, 128),
            local(512, 512),
            local(512, 512),
            local(512, 512),
            local(512, 512),
            local(2, 512, 512, dtype=f32),
            local(2, 128, 512, dtype=f32),
            local(2, 640, 512),
            local(2, 640, 512),
            local(512, 512),
            local(512, 512),
            local(512, 1536, dtype=f32),
            local(8, 512, dtype=i32),
            sems,
            local(512, 512),
            local(512, 512, dtype=i32),
        ],
        compiler_params=pltpu.CompilerParams(
            collective_id=0, has_side_effects=True, vmem_limit_bytes=60 << 20
        ),
        name="window",
    )(
        touched.transpose(0, 2, 1),
        src_pos[None, :],
        dst_owner.reshape(1, -1),
        dst_slot[None, :],
        neighbors.T,
        ev_time[None, :],
        neigh_time.T,
        time_freq[None, :],
        memory,
        *weights,
    )
    return pl.pallas_call(
        place_kernel,
        out_shape=(
            jax.ShapeDtypeStruct(emb.shape, bf16),
            jax.ShapeDtypeStruct(memory.shape, bf16),
        ),
        in_specs=[anyw] * 4,
        out_specs=(anyw, anyw),
        scratch_shapes=[
            local(8, 512, dtype=i32),
            local(512, 512),
            local(*memory.shape),
            local(*memory.shape),
            sems((3,)),
            sems((8,)),
            sems((8,)),
        ],
        compiler_params=pltpu.CompilerParams(vmem_limit_bytes=60 << 20),
        name="place",
    )(leader, fresh, memory, emb)


def solution(mesh):
    rows = P(("owner", "group"))
    in_specs = (rows,) * 8 + (P(),) * 9
    return jax.shard_map(
        per_device, mesh=mesh, in_specs=in_specs, out_specs=(rows, rows), check_vma=False
    )
```

```python
import jax
import jax.numpy as jnp
from jax import lax
from jax.experimental import pallas as pl
from jax.experimental.pallas import tpu as pltpu
from jax.sharding import PartitionSpec as P

HEADS = 2
MESH = pl.DeviceIdType.MESH
f32, bf16, i32 = jnp.float32, jnp.bfloat16, jnp.int32
COS = (
    0.9999992251396179,
    -0.499994158744812,
    0.041659727692604065,
    -0.00138586456887424,
    2.4201255655498244e-05,
    -2.196603787751883e-07,
)
NN = (((1,), (0,)), ((), ()))
NT = (((1,), (1,)), ((), ()))


def dot(a, b, dims=NN):
    return lax.dot_general(a, b, dims, preferred_element_type=f32)


def iota(shape, axis):
    return lax.broadcasted_iota(i32, shape, axis)


def hot(mask):
    return jnp.where(mask, 1.0, 0.0).astype(bf16)


def split(x):
    high = x.astype(bf16)
    return high, (x - high.astype(f32)).astype(bf16)


def take(x, index):
    return jnp.take_along_axis(x, index, axis=0, mode="promise_in_bounds")


def cosine(x):
    turns = jnp.floor(x * 0.15915494309189535 + 0.5)
    r = (x - turns * 6.28125) - turns * 0.0019353071795864769
    r = r * r
    y = COS[-1] * r + COS[-2]
    for c in COS[-3::-1]:
        y = y * r + c
    return y


def window_kernel(
    touched,
    src_pos,
    dst_owner,
    dst_slot,
    neighbors,
    ev_time,
    neigh_time,
    time_freq,
    memory_hbm,
    w_hidden_hbm,
    w_query_hbm,
    w_key_hbm,
    w_value_hbm,
    w_out_hbm,
    w_msg1_hbm,
    w_msg2_hbm,
    w_input_hbm,
    emb_hbm,
    fresh_hbm,
    lead_hbm,
    memory,
    w_hidden,
    w_query,
    w_key,
    w_value,
    w_out,
    w_msg1,
    w_msg2,
    w_input,
    load_sem,
    emb_sem,
    new_sem,
    ints,
    natural,
    note,
    notes,
    note_sem,
    own_sem,
    stage,
    outbox,
    inbox,
    table_sem,
    part_out,
    part_in,
    part_sem,
    code,
    picked,
    state,
    value_t,
    match_ref,
    share,
    ev_code,
    src_hot,
    dst_hot,
    dst_hot_t,
    table,
    full,
    query_code,
    spread_hi,
    spread_lo,
    emb,
    partial,
    gates,
    lead,
    lead_sem,
    fresh,
    finder,
    query_hi,
    query_lo,
    key_hi,
    key_lo,
    value_hi,
    value_lo,
    before,
):
    groups, owners = 8, 16
    n = groups * owners
    o, g = lax.axis_index("owner"), lax.axis_index("group")
    me = o * groups + g
    neigh, te, width = 16, 128, 512

    barrier = pltpu.get_barrier_semaphore()

    def greet(step, carry):
        peer = (me + step) & (n - 1)
        pl.semaphore_signal(
            barrier,
            inc=1,
            device_id=(peer // groups, peer & (groups - 1)),
            device_id_type=MESH,
        )
        return carry

    lax.fori_loop(1, n, greet, 0)
    loads = []
    for number, (source, target) in enumerate(
        (
            (memory_hbm, memory),
            (w_hidden_hbm, w_hidden),
            (w_value_hbm, w_value),
            (w_query_hbm, w_query),
            (w_key_hbm, w_key),
            (w_out_hbm, w_out),
            (w_msg1_hbm, w_msg1),
            (w_msg2_hbm, w_msg2),
            (w_input_hbm, w_input),
        )
    ):
        load = pltpu.make_async_copy(source, target, load_sem.at[number])
        load.start()
        loads.append(load)

    ints[0:neigh, :] = neighbors[...]
    ints[neigh : 2 * neigh, :] = ev_time[...] - neigh_time[...]
    ints[32:33, :] = src_pos[...]
    ints[33:34, :] = dst_owner[...] * 4 + dst_slot[...]
    ints[34:35, :] = ev_time[...]
    ints[35:40, :] = jnp.zeros((5, 512), i32)
    cols = ints[32:40, :].astype(f32).T.astype(i32)
    freq_row = time_freq[...]
    freq_col = jnp.broadcast_to(freq_row, (8, te)).T[:, 0:1]

    owner_hot = hot(iota((n, 512), 0) == dst_owner[...])
    slot_hot = hot(iota((n, 512), 0) == dst_slot[...] + 4)
    natural[...] = dot(owner_hot, slot_hot, NT).astype(i32)
    wanted = jnp.concatenate([touched[0], touched[0]], axis=0).astype(f32)
    natural[:, 0:4] = wanted.T[:, 0:4].astype(i32)
    note[:, 0, :] = natural[...]
    pl.semaphore_wait(barrier, n - 1)

    def send_all(source, target, send_sem, recv_sem):
        def send(step, carry):
            peer = (me + step) & (n - 1)
            pltpu.make_async_remote_copy(
                src_ref=source.at[peer],
                dst_ref=target.at[me],
                send_sem=send_sem,
                recv_sem=recv_sem,
                device_id=(peer // groups, peer & (groups - 1)),
                device_id_type=MESH,
            ).start()
            return carry

        lax.fori_loop(1, n, send, 0)

    def all_sent(source, target, send_sem, recv_sem):
        return pltpu.make_async_remote_copy(
            src_ref=source.at[pl.ds(0, n - 1)],
            dst_ref=target.at[pl.ds(0, n - 1)],
            send_sem=send_sem,
            recv_sem=recv_sem,
            device_id=(o, (g + 1) & (groups - 1)),
            device_id_type=MESH,
        )

    own = pltpu.make_async_copy(note.at[me], notes.at[me], own_sem.at[0])
    own.start()
    send_all(note, notes, note_sem.at[0], note_sem.at[1])

    def make_codes(first):
        def codes(k, carry):
            for i in range(te // 32):
                rows = slice(i * 32, i * 32 + 32)
                code[k, rows, :] = cosine(freq_col[rows] * delta).astype(bf16).astype(f32)
            return carry

        for k in range(first, first + neigh // 2):
            delta = ints[k + neigh : k + neigh + 1, :].astype(f32)
            codes(k, 0)

    make_codes(0)
    make_codes(neigh // 2)

    def find(piece, carry):
        lanes = pl.ds(pl.multiple_of(piece * 128, 128), 128)
        near = ints[0:neigh, lanes]
        near8 = [jnp.broadcast_to(near[k : k + 1, :], (8, 128)) for k in range(neigh)]
        sub = iota((8, 128), 0)

        def scan(i, carry):
            for u in range(4):
                base = pl.multiple_of(i * 32 + u * 8, 8)
                which = jnp.full((8, 128), neigh, i32)
                for k in range(neigh):
                    which = jnp.where(sub + base == near8[k], k, which)
                finder[pl.ds(base, 8), lanes] = which
            return carry

        lax.fori_loop(0, 16, scan, 0)
        return carry

    lax.fori_loop(0, 4, find, 0)
    own.wait()
    all_sent(note, notes, note_sem.at[0], note_sem.at[1]).wait()
    known = notes[:, 0, :]
    known_t = known.astype(f32).T.astype(i32)

    loads[0].wait()
    for s in range(4):
        rows = dot(hot(iota((n, 2048), 1) == known[:, s : s + 1]), memory[...])
        picked[s * n : (s + 1) * n, :] = rows.astype(bf16)
        for c in range(4):
            stage[pl.ds(s * 4 + c, n, stride=16), :] = rows[:, c * 128 : (c + 1) * 128]
    outbox[...] = stage[...].astype(bf16).reshape(n, 16, 128)

    own = pltpu.make_async_copy(outbox.at[me], inbox.at[me], own_sem.at[2])
    own.start()
    send_all(outbox, inbox, table_sem.at[0], table_sem.at[1])

    loads[1].wait()
    state[...] = dot(picked[...], w_hidden[...])
    loads[2].wait()
    value_t[...] = w_value[...].astype(f32).T.astype(bf16)
    value_hi[:, width:] = value_t[:, width:]
    asked_col = jnp.concatenate([known[:, s : s + 1] for s in range(4)], axis=0)
    count_col = jnp.concatenate([known[:, s + 4 : s + 5] for s in range(4)], axis=0)
    asked_row = jnp.concatenate([known_t[s : s + 1, :] for s in range(4)], axis=1)
    count_row = jnp.concatenate([known_t[s + 4 : s + 5, :] for s in range(4)], axis=1)
    match = asked_col == asked_row
    match_ref[...] = hot(match)
    number = jnp.sum(jnp.where(match, count_row.astype(f32), 0.0), axis=1, keepdims=True)
    share[...] = jnp.broadcast_to(1.0 / jnp.maximum(number, 1.0), share.shape)
    number_row = jnp.sum(jnp.where(match, count_col.astype(f32), 0.0), axis=0, keepdims=True)
    earlier = match & (iota((512, 512), 0) < iota((512, 512), 1))
    earlier = jnp.sum(jnp.where(earlier, 1.0, 0.0), axis=0, keepdims=True)
    leader = jnp.where((earlier == 0.0) & (number_row > 0.0), asked_row, -1)
    lead[...] = jnp.broadcast_to(leader, lead.shape)
    lead_copy = pltpu.make_async_copy(lead, lead_hbm, lead_sem)
    lead_copy.start()
    ev_code[...] = cosine(cols[:, 2:3].astype(f32) * freq_row).astype(bf16)
    src_hot[...] = hot(iota((512, 512), 1) == cols[:, 0:1])
    dst_hot[...] = hot(iota((512, 512), 1) == cols[:, 1:2])
    dst_hot_t[...] = hot(iota((512, 512), 0) == ints[33:34, :])

    own.wait()
    all_sent(outbox, inbox, table_sem.at[0], table_sem.at[1]).wait()
    stage[...] = inbox[...].reshape(n * 16, 128).astype(f32)
    for c in range(4):
        table[:, c * 128 : (c + 1) * 128] = stage[pl.ds(c, 512, stride=4), :].astype(bf16)

    dst_mem = dot(dst_hot[...], table[...])
    loads[3].wait()
    loads[4].wait()
    query = dot(dst_mem.astype(bf16), w_query[...]) * (1.0 / 16.0)
    query_hi[...], query_lo[...] = split(query)
    key_hi[...], key_lo[...] = split(dot(table[...], w_key[:width, :]))
    for h in range(HEADS):
        part = slice(h * 256, h * 256 + 256)
        query_code[h] = dot(w_key[width:, part], query_hi[:, part], NT) + dot(
            w_key[width:, part], query_lo[:, part], NT
        )
        full[h] = (
            dot(key_hi[:, part], query_hi[:, part], NT)
            + dot(key_hi[:, part], query_lo[:, part], NT)
            + dot(key_lo[:, part], query_hi[:, part], NT)
        )
    loads[6].wait()

    def attend(piece, carry):
        lanes = pl.ds(pl.multiple_of(piece * 128, 128), 128)
        value_hi[lanes, :width], value_lo[lanes, :] = split(
            dot(value_t[lanes, :width], table[...], NT)
        )
        src_mem = dot(src_hot[lanes, :], table[...]).astype(bf16)
        before[lanes, :] = dot(src_mem, w_msg1[:width, :]) + dot(
            ev_code[lanes, :], w_msg1[2 * width :, :]
        )
        near = ints[0:neigh, lanes]
        fine = [near[b * 8 : b * 8 + 8, :] & 7 for b in range(2)]
        coarse = [near[b * 8 : b * 8 + 8, :] >> 3 for b in range(2)]

        zero = jnp.zeros((8, 128), f32)
        def timed(i, sums):
            sums = list(sums)
            rows = pl.ds(pl.multiple_of(i * 8, 8), 8)
            mine = [query_code[h, rows, lanes] for h in range(HEADS)]
            for k in range(neigh):
                one = code[k, rows, lanes]
                for h in range(HEADS):
                    sums[h * neigh + k] += one * mine[h]
            return tuple(sums)

        sums = lax.fori_loop(0, te // 8, timed, (zero,) * (HEADS * neigh), unroll=16)
        def look(i, found):
            found = list(found)
            for u in range(8):
                base = pl.multiple_of(i * 64 + u * 8, 8)
                for b in range(2):
                    mask = coarse[b] == i * 8 + u
                    for h in range(HEADS):
                        taken = take(full[h, pl.ds(base, 8), lanes], fine[b])
                        found[h * 2 + b] = jnp.where(mask, taken, found[h * 2 + b])
            return tuple(found)

        found = lax.fori_loop(0, 8, look, (zero,) * (2 * HEADS), unroll=8)

        whole = []
        weights = []
        for h in range(HEADS):
            score = jnp.concatenate(
                [
                    jnp.sum(sums[h * neigh + k], axis=0, keepdims=True)
                    for k in range(neigh)
                ],
                axis=0,
            ) + jnp.concatenate(found[h * 2 : h * 2 + 2], axis=0)
            score = jnp.exp(score - jnp.max(score, axis=0, keepdims=True))
            weight = score / jnp.sum(score, axis=0, keepdims=True)
            total = jnp.zeros((neigh, 128), f32)
            for k in range(neigh):
                total += jnp.where(near == near[k : k + 1, :], weight[k : k + 1, :], 0.0)
            weights.append(weight)
            whole.append([total[0:8, :], total[8:16, :]])

        def put(i, carry):
            for u in range(4):
                base = pl.multiple_of(i * 64 + u * 16, 16)
                both = [[], []]
                for v in range(2):
                    which = finder[pl.ds(base + v * 8, 8), lanes]
                    fine = which & 7
                    for h in range(HEADS):
                        first = jnp.where(which < 8, take(whole[h][0], fine), 0.0)
                        second = take(whole[h][1], fine)
                        both[h].append(
                            jnp.where((which & 24) == 8, second, first)
                        )
                for h in range(HEADS):
                    high, low = split(jnp.concatenate(both[h], axis=0))
                    spread_hi[h, pl.ds(base, 16), lanes] = high
                    spread_lo[h, pl.ds(base, 16), lanes] = low
            return carry

        lax.fori_loop(0, 8, put, 0, unroll=8)
        spread = [
            [jnp.broadcast_to(weights[h][k : k + 1, :], (8, 128)) for k in range(neigh)]
            for h in range(HEADS)
        ]

        def mix(i, carry):
            base = pl.multiple_of(i * 16, 16)
            both = [[], []]
            for v in range(2):
                mixed = [zero] * HEADS
                for k in range(neigh):
                    one = code[k, pl.ds(base + v * 8, 8), lanes]
                    for h in range(HEADS):
                        mixed[h] += one * spread[h][k]
                for h in range(HEADS):
                    both[h].append(mixed[h])
            for h in range(HEADS):
                high, low = split(jnp.concatenate(both[h], axis=0))
                spread_hi[h, pl.ds(width + base, 16), lanes] = high
                spread_lo[h, pl.ds(width + base, 16), lanes] = low
            return carry

        lax.fori_loop(0, te // 16, mix, 0, unroll=8)
        return carry

    lax.fori_loop(0, 4, attend, 0)
    att = []
    for h in range(HEADS):
        part = slice(h * 256, h * 256 + 256)
        att.append(
            dot(value_hi[part, :], spread_hi[h])
            + dot(value_hi[part, :], spread_lo[h])
            + dot(value_lo[part, :], spread_hi[h, :width, :])
        )
    att = jnp.concatenate(att, axis=0).T.astype(bf16)
    loads[5].wait()
    emb[...] = (dst_mem + dot(att, w_out[...])).astype(bf16)
    emb_copy = pltpu.make_async_copy(emb, emb_hbm, emb_sem)
    emb_copy.start()
    hidden = before[...] + dot(emb[...], w_msg1[width : 2 * width, :])
    hidden = jnp.maximum(hidden, 0.0).astype(bf16)
    loads[7].wait()
    owns = []
    for half in range(2):
        part = slice(half * 512, half * 512 + 512)
        message = dot(hidden, w_msg2[:, part]).astype(bf16)
        sums = dot(dst_hot_t[...], message)
        for c in range(4):
            stage[pl.ds(c, 512, stride=4), :] = sums[:, c * 128 : (c + 1) * 128]
        part_out[half] = stage[...].astype(bf16).reshape(n, 16, 128)
        own = pltpu.make_async_copy(
            part_out.at[half, me], part_in.at[half, me], own_sem.at[3 + half]
        )
        own.start()
        owns.append(own)
        send_all(
            part_out.at[half], part_in.at[half], part_sem.at[2 * half], part_sem.at[2 * half + 1]
        )
    emb_copy.wait()
    loads[8].wait()
    for half in range(2):
        owns[half].wait()
        all_sent(
            part_out.at[half], part_in.at[half], part_sem.at[2 * half], part_sem.at[2 * half + 1]
        ).wait()
        stage[...] = part_in[half].reshape(n * 16, 128).astype(f32)
        for s in range(4):
            for c in range(4):
                partial[s * n : (s + 1) * n, c * 128 : (c + 1) * 128] = stage[
                    pl.ds(s * 4 + c, n, stride=16), :
                ].astype(bf16)
        total = dot(match_ref[...], partial[...])
        agg = jnp.concatenate(
            [total[:, c * 128 : (c + 1) * 128] * share[...] for c in range(4)], axis=1
        ).astype(bf16)
        gate = dot(agg, w_input[half * 512 : half * 512 + 512, :])
        if half == 0:
            gates[...] = gate
        else:
            gates[...] += gate

    def update_rows(i, carry):
        rows = pl.ds(pl.multiple_of(i * 64, 64), 64)
        reset = jax.nn.sigmoid(gates[rows, 0:width] + state[rows, 0:width])
        update = jax.nn.sigmoid(
            gates[rows, width : 2 * width] + state[rows, width : 2 * width]
        )
        new = jnp.tanh(gates[rows, 2 * width :] + reset * state[rows, 2 * width :])
        old = picked[rows, :].astype(f32)
        fresh[rows, :] = ((1.0 - update) * new + update * old).astype(bf16)
        return carry

    lax.fori_loop(0, 8, update_rows, 0)

    fresh_copy = pltpu.make_async_copy(fresh, fresh_hbm, new_sem)
    fresh_copy.start()
    lead_copy.wait()
    fresh_copy.wait()


def place_kernel(
    leader_hbm,
    fresh_hbm,
    memory_hbm,
    emb_hbm,
    emb_out,
    new_hbm,
    leader,
    fresh,
    memory,
    moved,
    emb,
    sem,
    in_sem,
    out_sem,
):
    leader_copy = pltpu.make_async_copy(leader_hbm, leader, sem.at[1])
    leader_copy.start()
    fresh_copy = pltpu.make_async_copy(fresh_hbm, fresh, sem.at[2])
    fresh_copy.start()
    blocks = []
    for i in range(8):
        rows = pl.ds(i * 256, 256)
        block = pltpu.make_async_copy(memory_hbm.at[rows], memory.at[rows], in_sem.at[i])
        block.start()
        blocks.append(block)
    emb_in = pltpu.make_async_copy(emb_hbm, emb, sem.at[0])
    emb_in.start()
    leader_copy.wait()
    outs = []
    for i in range(8):
        rows = slice(i * 256, i * 256 + 256)
        mask = iota((256, 512), 0) + i * 256 == leader[0:1, :]
        hit = jnp.max(jnp.where(mask, 1.0, 0.0), axis=1, keepdims=True)
        if i == 0:
            fresh_copy.wait()
        new = dot(hot(mask), fresh[...])
        blocks[i].wait()
        moved[rows, :] = jnp.where(hit > 0.0, new, memory[rows, :].astype(f32)).astype(bf16)
        rows = pl.ds(i * 256, 256)
        out = pltpu.make_async_copy(moved.at[rows], new_hbm.at[rows], out_sem.at[i])
        out.start()
        outs.append(out)
        if i == 3:
            emb_in.wait()
            emb_copy = pltpu.make_async_copy(emb, emb_out, sem.at[3])
            emb_copy.start()
    emb_copy.wait()
    for out in outs:
        out.wait()


def per_device(
    memory,
    touched,
    src_pos,
    dst_owner,
    dst_slot,
    neighbors,
    ev_time,
    neigh_time,
    time_freq,
    w_query,
    w_key,
    w_value,
    w_out,
    w_msg1,
    w_msg2,
    w_input,
    w_hidden,
):
    vmem = pl.BlockSpec(memory_space=pltpu.VMEM)
    anyw = pl.BlockSpec(memory_space=pl.ANY)
    weights = (w_hidden, w_query, w_key, w_value, w_out, w_msg1, w_msg2, w_input)

    def local(*shape, dtype=bf16):
        return pltpu.VMEM(shape, dtype)

    sems = pltpu.SemaphoreType.DMA
    emb, fresh, leader = pl.pallas_call(
        window_kernel,
        out_shape=(
            jax.ShapeDtypeStruct((512, 512), bf16),
            jax.ShapeDtypeStruct((512, 512), bf16),
            jax.ShapeDtypeStruct((8, 512), i32),
        ),
        in_specs=[vmem] * 8 + [anyw] * 9,
        out_specs=(anyw,) * 3,
        scratch_shapes=[
            local(*memory.shape),
            *[local(*w.shape) for w in weights],
            sems((9,)),
            sems,
            sems,
            local(40, 512, dtype=i32),
            local(128, 128, dtype=i32),
            local(128, 1, 128, dtype=i32),
            local(128, 1, 128, dtype=i32),
            sems((2,)),
            sems((5,)),
            local(2048, 128, dtype=f32),
            local(128, 16, 128),
            local(128, 16, 128),
            sems((2,)),
            local(2, 128, 16, 128),
            local(2, 128, 16, 128),
            sems((4,)),
            local(16, 128, 512, dtype=f32),
            local(512, 512),
            local(512, 1536, dtype=f32),
            local(512, 640),
            local(512, 512),
            local(512, 128, dtype=f32),
            local(512, 128),
            local(512, 512),
            local(512, 512),
            local(512, 512),
            local(512, 512),
            local(2, 512, 512, dtype=f32),
            local(2, 128, 512, dtype=f32),
            local(2, 640, 512),
            local(2, 640, 512),
            local(512, 512),
            local(512, 512),
            local(512, 1536, dtype=f32),
            local(8, 512, dtype=i32),
            sems,
            local(512, 512),
            local(512, 512, dtype=i32),
            *[local(512, 512)] * 4,
            local(512, 640),
            local(512, 512),
            local(512, 1024, dtype=f32),
        ],
        compiler_params=pltpu.CompilerParams(
            collective_id=0, has_side_effects=True, vmem_limit_bytes=60 << 20
        ),
        name="window",
    )(
        touched.transpose(0, 2, 1),
        src_pos[None, :],
        dst_owner.reshape(1, -1),
        dst_slot[None, :],
        neighbors.T,
        ev_time[None, :],
        neigh_time.T,
        time_freq[None, :],
        memory,
        *weights,
    )
    return pl.pallas_call(
        place_kernel,
        out_shape=(
            jax.ShapeDtypeStruct(emb.shape, bf16),
            jax.ShapeDtypeStruct(memory.shape, bf16),
        ),
        in_specs=[anyw] * 4,
        out_specs=(anyw, anyw),
        scratch_shapes=[
            local(8, 512, dtype=i32),
            local(512, 512),
            local(*memory.shape),
            local(*memory.shape),
            local(512, 512),
            sems((4,)),
            sems((8,)),
            sems((8,)),
        ],
        compiler_params=pltpu.CompilerParams(vmem_limit_bytes=60 << 20),
        name="place",
    )(leader, fresh, memory, emb)


def solution(mesh):
    rows = P(("owner", "group"))
    in_specs = (rows,) * 8 + (P(),) * 9
    return jax.shard_map(
        per_device, mesh=mesh, in_specs=in_specs, out_specs=(rows, rows), check_vma=False
    )
```

```python
import jax
import jax.numpy as jnp
from jax import lax
from jax.experimental import pallas as pl
from jax.experimental.pallas import tpu as pltpu
from jax.sharding import PartitionSpec as P

HEADS = 2
MESH = pl.DeviceIdType.MESH
f32, bf16, i32 = jnp.float32, jnp.bfloat16, jnp.int32
COS = (
    0.9999992251396179,
    -0.499994158744812,
    0.041659727692604065,
    -0.00138586456887424,
    2.4201255655498244e-05,
    -2.196603787751883e-07,
)
NN = (((1,), (0,)), ((), ()))
NT = (((1,), (1,)), ((), ()))


def dot(a, b, dims=NN):
    return lax.dot_general(a, b, dims, preferred_element_type=f32)


def iota(shape, axis):
    return lax.broadcasted_iota(i32, shape, axis)


def hot(mask):
    return jnp.where(mask, 1.0, 0.0).astype(bf16)


def split(x):
    high = x.astype(bf16)
    return high, (x - high.astype(f32)).astype(bf16)


def take(x, index):
    return jnp.take_along_axis(x, index, axis=0, mode="promise_in_bounds")


def cosine(x):
    turns = jnp.floor(x * 0.15915494309189535 + 0.5)
    r = (x - turns * 6.28125) - turns * 0.0019353071795864769
    r = r * r
    y = COS[-1] * r + COS[-2]
    for c in COS[-3::-1]:
        y = y * r + c
    return y


def window_kernel(
    touched,
    src_pos,
    dst_owner,
    dst_slot,
    neighbors,
    ev_time,
    neigh_time,
    time_freq,
    memory_hbm,
    w_hidden_hbm,
    w_query_hbm,
    w_key_hbm,
    w_value_hbm,
    w_out_hbm,
    w_msg1_hbm,
    w_msg2_hbm,
    w_input_hbm,
    joint_hbm,
    memory,
    w_hidden,
    w_query,
    w_key,
    w_value,
    w_out,
    w_msg1,
    w_msg2,
    w_input,
    load_sem,
    emb_sem,
    new_sem,
    ints,
    natural,
    note,
    notes,
    note_sem,
    own_sem,
    stage,
    outbox,
    inbox,
    table_sem,
    part_out,
    part_in,
    part_sem,
    code,
    picked,
    state,
    value_t,
    match_ref,
    share,
    ev_code,
    src_hot,
    dst_hot,
    dst_hot_t,
    table,
    full,
    query_code,
    spread_hi,
    spread_lo,
    emb,
    partial,
    gates,
    lead,
    lead_sem,
    fresh,
    finder,
    query_hi,
    query_lo,
    key_hi,
    key_lo,
    value_hi,
    value_lo,
    before,
):
    groups, owners = 8, 16
    n = groups * owners
    o, g = lax.axis_index("owner"), lax.axis_index("group")
    me = o * groups + g
    neigh, te, width = 16, 128, 512

    barrier = pltpu.get_barrier_semaphore()

    def greet(step, carry):
        peer = (me + step) & (n - 1)
        pl.semaphore_signal(
            barrier,
            inc=1,
            device_id=(peer // groups, peer & (groups - 1)),
            device_id_type=MESH,
        )
        return carry

    lax.fori_loop(1, n, greet, 0)
    loads = []
    for number, (source, target) in enumerate(
        (
            (memory_hbm, memory),
            (w_hidden_hbm, w_hidden),
            (w_value_hbm, w_value),
            (w_query_hbm, w_query),
            (w_key_hbm, w_key),
            (w_out_hbm, w_out),
            (w_msg1_hbm, w_msg1),
            (w_msg2_hbm, w_msg2),
            (w_input_hbm, w_input),
        )
    ):
        load = pltpu.make_async_copy(source, target, load_sem.at[number])
        load.start()
        loads.append(load)

    ints[0:neigh, :] = neighbors[...]
    ints[neigh : 2 * neigh, :] = ev_time[...] - neigh_time[...]
    ints[32:33, :] = src_pos[...]
    ints[33:34, :] = dst_owner[...] * 4 + dst_slot[...]
    ints[34:35, :] = ev_time[...]
    ints[35:40, :] = jnp.zeros((5, 512), i32)
    cols = ints[32:40, :].astype(f32).T.astype(i32)
    freq_row = time_freq[...]
    freq_col = jnp.broadcast_to(freq_row, (8, te)).T[:, 0:1]

    owner_hot = hot(iota((n, 512), 0) == dst_owner[...])
    slot_hot = hot(iota((n, 512), 0) == dst_slot[...] + 4)
    natural[...] = dot(owner_hot, slot_hot, NT).astype(i32)
    wanted = jnp.concatenate([touched[0], touched[0]], axis=0).astype(f32)
    natural[:, 0:4] = wanted.T[:, 0:4].astype(i32)
    note[:, 0, :] = natural[...]
    pl.semaphore_wait(barrier, n - 1)

    def send_all(source, target, send_sem, recv_sem):
        def send(step, carry):
            peer = (me + step) & (n - 1)
            pltpu.make_async_remote_copy(
                src_ref=source.at[peer],
                dst_ref=target.at[me],
                send_sem=send_sem,
                recv_sem=recv_sem,
                device_id=(peer // groups, peer & (groups - 1)),
                device_id_type=MESH,
            ).start()
            return carry

        lax.fori_loop(1, n, send, 0)

    def all_sent(source, target, send_sem, recv_sem):
        return pltpu.make_async_remote_copy(
            src_ref=source.at[pl.ds(0, n - 1)],
            dst_ref=target.at[pl.ds(0, n - 1)],
            send_sem=send_sem,
            recv_sem=recv_sem,
            device_id=(o, (g + 1) & (groups - 1)),
            device_id_type=MESH,
        )

    own = pltpu.make_async_copy(note.at[me], notes.at[me], own_sem.at[0])
    own.start()
    send_all(note, notes, note_sem.at[0], note_sem.at[1])

    def make_codes(first):
        def codes(k, carry):
            for i in range(te // 32):
                rows = slice(i * 32, i * 32 + 32)
                code[k, rows, :] = cosine(freq_col[rows] * delta).astype(bf16).astype(f32)
            return carry

        for k in range(first, first + neigh // 2):
            delta = ints[k + neigh : k + neigh + 1, :].astype(f32)
            codes(k, 0)

    make_codes(0)
    make_codes(neigh // 2)

    def find(piece, carry):
        lanes = pl.ds(pl.multiple_of(piece * 128, 128), 128)
        near = ints[0:neigh, lanes]
        near8 = [jnp.broadcast_to(near[k : k + 1, :], (8, 128)) for k in range(neigh)]
        sub = iota((8, 128), 0)

        def scan(i, carry):
            for u in range(4):
                base = pl.multiple_of(i * 32 + u * 8, 8)
                which = jnp.full((8, 128), neigh, i32)
                for k in range(neigh):
                    which = jnp.where(sub + base == near8[k], k, which)
                finder[pl.ds(base, 8), lanes] = which
            return carry

        lax.fori_loop(0, 16, scan, 0)
        return carry

    lax.fori_loop(0, 4, find, 0)
    own.wait()
    all_sent(note, notes, note_sem.at[0], note_sem.at[1]).wait()
    known = notes[:, 0, :]
    known_t = known.astype(f32).T.astype(i32)

    loads[0].wait()
    for s in range(4):
        rows = dot(hot(iota((n, 2048), 1) == known[:, s : s + 1]), memory[...])
        picked[s * n : (s + 1) * n, :] = rows.astype(bf16)
        for c in range(4):
            stage[pl.ds(s * 4 + c, n, stride=16), :] = rows[:, c * 128 : (c + 1) * 128]
    outbox[...] = stage[...].astype(bf16).reshape(n, 16, 128)

    own = pltpu.make_async_copy(outbox.at[me], inbox.at[me], own_sem.at[2])
    own.start()
    send_all(outbox, inbox, table_sem.at[0], table_sem.at[1])

    loads[1].wait()
    state[...] = dot(picked[...], w_hidden[...])
    loads[2].wait()
    value_t[...] = w_value[...].astype(f32).T.astype(bf16)
    value_hi[:, width:] = value_t[:, width:]
    asked_col = jnp.concatenate([known[:, s : s + 1] for s in range(4)], axis=0)
    count_col = jnp.concatenate([known[:, s + 4 : s + 5] for s in range(4)], axis=0)
    asked_row = jnp.concatenate([known_t[s : s + 1, :] for s in range(4)], axis=1)
    count_row = jnp.concatenate([known_t[s + 4 : s + 5, :] for s in range(4)], axis=1)
    match = asked_col == asked_row
    match_ref[...] = hot(match)
    number = jnp.sum(jnp.where(match, count_row.astype(f32), 0.0), axis=1, keepdims=True)
    share[...] = jnp.broadcast_to(1.0 / jnp.maximum(number, 1.0), share.shape)
    number_row = jnp.sum(jnp.where(match, count_col.astype(f32), 0.0), axis=0, keepdims=True)
    earlier = match & (iota((512, 512), 0) < iota((512, 512), 1))
    earlier = jnp.sum(jnp.where(earlier, 1.0, 0.0), axis=0, keepdims=True)
    leader = jnp.where((earlier == 0.0) & (number_row > 0.0), asked_row, -1)
    row = jnp.broadcast_to(leader + 64, lead.shape)
    row = jnp.where(iota(lead.shape, 0) == 0, row >> 6, row & 63)
    lead[...] = row.astype(f32).astype(bf16)
    lead_copy = pltpu.make_async_copy(lead, joint_hbm.at[pl.ds(1024, 16)], lead_sem)
    lead_copy.start()
    ev_code[...] = cosine(cols[:, 2:3].astype(f32) * freq_row).astype(bf16)
    src_hot[...] = hot(iota((512, 512), 1) == cols[:, 0:1])
    dst_hot[...] = hot(iota((512, 512), 1) == cols[:, 1:2])
    dst_hot_t[...] = hot(iota((512, 512), 0) == ints[33:34, :])

    own.wait()
    all_sent(outbox, inbox, table_sem.at[0], table_sem.at[1]).wait()
    stage[...] = inbox[...].reshape(n * 16, 128).astype(f32)
    for c in range(4):
        table[:, c * 128 : (c + 1) * 128] = stage[pl.ds(c, 512, stride=4), :].astype(bf16)

    dst_mem = dot(dst_hot[...], table[...])
    loads[3].wait()
    loads[4].wait()
    query = dot(dst_mem.astype(bf16), w_query[...]) * (1.0 / 16.0)
    query_hi[...], query_lo[...] = split(query)
    key_hi[...], key_lo[...] = split(dot(table[...], w_key[:width, :]))
    for h in range(HEADS):
        part = slice(h * 256, h * 256 + 256)
        query_code[h] = dot(w_key[width:, part], query_hi[:, part], NT) + dot(
            w_key[width:, part], query_lo[:, part], NT
        )
        full[h] = (
            dot(key_hi[:, part], query_hi[:, part], NT)
            + dot(key_hi[:, part], query_lo[:, part], NT)
            + dot(key_lo[:, part], query_hi[:, part], NT)
        )
    loads[6].wait()

    def attend(piece, carry):
        lanes = pl.ds(pl.multiple_of(piece * 128, 128), 128)
        value_hi[lanes, :width], value_lo[lanes, :] = split(
            dot(value_t[lanes, :width], table[...], NT)
        )
        src_mem = dot(src_hot[lanes, :], table[...]).astype(bf16)
        before[lanes, :] = dot(src_mem, w_msg1[:width, :]) + dot(
            ev_code[lanes, :], w_msg1[2 * width :, :]
        )
        near = ints[0:neigh, lanes]
        fine = [near[b * 8 : b * 8 + 8, :] & 7 for b in range(2)]
        coarse = [near[b * 8 : b * 8 + 8, :] >> 3 for b in range(2)]

        zero = jnp.zeros((8, 128), f32)
        def timed(i, sums):
            sums = list(sums)
            rows = pl.ds(pl.multiple_of(i * 8, 8), 8)
            mine = [query_code[h, rows, lanes] for h in range(HEADS)]
            for k in range(neigh):
                one = code[k, rows, lanes]
                for h in range(HEADS):
                    sums[h * neigh + k] += one * mine[h]
            return tuple(sums)

        sums = lax.fori_loop(0, te // 8, timed, (zero,) * (HEADS * neigh), unroll=16)
        def look(i, found):
            found = list(found)
            for u in range(8):
                base = pl.multiple_of(i * 64 + u * 8, 8)
                for b in range(2):
                    mask = coarse[b] == i * 8 + u
                    for h in range(HEADS):
                        taken = take(full[h, pl.ds(base, 8), lanes], fine[b])
                        found[h * 2 + b] = jnp.where(mask, taken, found[h * 2 + b])
            return tuple(found)

        found = lax.fori_loop(0, 8, look, (zero,) * (2 * HEADS), unroll=8)

        whole = []
        weights = []
        for h in range(HEADS):
            score = jnp.concatenate(
                [
                    jnp.sum(sums[h * neigh + k], axis=0, keepdims=True)
                    for k in range(neigh)
                ],
                axis=0,
            ) + jnp.concatenate(found[h * 2 : h * 2 + 2], axis=0)
            score = jnp.exp(score - jnp.max(score, axis=0, keepdims=True))
            weight = score / jnp.sum(score, axis=0, keepdims=True)
            total = jnp.zeros((neigh, 128), f32)
            for k in range(neigh):
                total += jnp.where(near == near[k : k + 1, :], weight[k : k + 1, :], 0.0)
            weights.append(weight)
            whole.append([total[0:8, :], total[8:16, :]])

        def put(i, carry):
            for u in range(4):
                base = pl.multiple_of(i * 64 + u * 16, 16)
                both = [[], []]
                for v in range(2):
                    which = finder[pl.ds(base + v * 8, 8), lanes]
                    fine = which & 7
                    for h in range(HEADS):
                        first = jnp.where(which < 8, take(whole[h][0], fine), 0.0)
                        second = take(whole[h][1], fine)
                        both[h].append(
                            jnp.where((which & 24) == 8, second, first)
                        )
                for h in range(HEADS):
                    high, low = split(jnp.concatenate(both[h], axis=0))
                    spread_hi[h, pl.ds(base, 16), lanes] = high
                    spread_lo[h, pl.ds(base, 16), lanes] = low
            return carry

        lax.fori_loop(0, 8, put, 0, unroll=8)
        spread = [
            [jnp.broadcast_to(weights[h][k : k + 1, :], (8, 128)) for k in range(neigh)]
            for h in range(HEADS)
        ]

        def mix(i, carry):
            base = pl.multiple_of(i * 16, 16)
            both = [[], []]
            for v in range(2):
                mixed = [zero] * HEADS
                for k in range(neigh):
                    one = code[k, pl.ds(base + v * 8, 8), lanes]
                    for h in range(HEADS):
                        mixed[h] += one * spread[h][k]
                for h in range(HEADS):
                    both[h].append(mixed[h])
            for h in range(HEADS):
                high, low = split(jnp.concatenate(both[h], axis=0))
                spread_hi[h, pl.ds(width + base, 16), lanes] = high
                spread_lo[h, pl.ds(width + base, 16), lanes] = low
            return carry

        lax.fori_loop(0, te // 16, mix, 0, unroll=8)
        return carry

    lax.fori_loop(0, 4, attend, 0)
    att = []
    for h in range(HEADS):
        part = slice(h * 256, h * 256 + 256)
        att.append(
            dot(value_hi[part, :], spread_hi[h])
            + dot(value_hi[part, :], spread_lo[h])
            + dot(value_lo[part, :], spread_hi[h, :width, :])
        )
    att = jnp.concatenate(att, axis=0).T.astype(bf16)
    loads[5].wait()
    emb[...] = (dst_mem + dot(att, w_out[...])).astype(bf16)
    emb_copy = pltpu.make_async_copy(emb, joint_hbm.at[pl.ds(0, 512)], emb_sem)
    emb_copy.start()
    hidden = before[...] + dot(emb[...], w_msg1[width : 2 * width, :])
    hidden = jnp.maximum(hidden, 0.0).astype(bf16)
    loads[7].wait()
    owns = []
    for half in range(2):
        part = slice(half * 512, half * 512 + 512)
        message = dot(hidden, w_msg2[:, part]).astype(bf16)
        sums = dot(dst_hot_t[...], message)
        for c in range(4):
            stage[pl.ds(c, 512, stride=4), :] = sums[:, c * 128 : (c + 1) * 128]
        part_out[half] = stage[...].astype(bf16).reshape(n, 16, 128)
        own = pltpu.make_async_copy(
            part_out.at[half, me], part_in.at[half, me], own_sem.at[3 + half]
        )
        own.start()
        owns.append(own)
        send_all(
            part_out.at[half], part_in.at[half], part_sem.at[2 * half], part_sem.at[2 * half + 1]
        )
    emb_copy.wait()
    loads[8].wait()
    for half in range(2):
        owns[half].wait()
        all_sent(
            part_out.at[half], part_in.at[half], part_sem.at[2 * half], part_sem.at[2 * half + 1]
        ).wait()
        stage[...] = part_in[half].reshape(n * 16, 128).astype(f32)
        for s in range(4):
            for c in range(4):
                partial[s * n : (s + 1) * n, c * 128 : (c + 1) * 128] = stage[
                    pl.ds(s * 4 + c, n, stride=16), :
                ].astype(bf16)
        total = dot(match_ref[...], partial[...])
        agg = jnp.concatenate(
            [total[:, c * 128 : (c + 1) * 128] * share[...] for c in range(4)], axis=1
        ).astype(bf16)
        gate = dot(agg, w_input[half * 512 : half * 512 + 512, :])
        if half == 0:
            gates[...] = gate
        else:
            gates[...] += gate

    def update_rows(i, carry):
        rows = pl.ds(pl.multiple_of(i * 64, 64), 64)
        reset = jax.nn.sigmoid(gates[rows, 0:width] + state[rows, 0:width])
        update = jax.nn.sigmoid(
            gates[rows, width : 2 * width] + state[rows, width : 2 * width]
        )
        new = jnp.tanh(gates[rows, 2 * width :] + reset * state[rows, 2 * width :])
        old = picked[rows, :].astype(f32)
        fresh[rows, :] = ((1.0 - update) * new + update * old).astype(bf16)
        return carry

    lax.fori_loop(0, 8, update_rows, 0)

    fresh_copy = pltpu.make_async_copy(fresh, joint_hbm.at[pl.ds(512, 512)], new_sem)
    fresh_copy.start()
    lead_copy.wait()
    fresh_copy.wait()


def place_kernel(joint, memory, emb_out, new_hbm, moved, emb_sem, out_sem):
    emb_copy = pltpu.make_async_copy(joint.at[pl.ds(0, 512)], emb_out, emb_sem)
    emb_copy.start()
    row = joint[1024:1040, :].astype(f32)
    leader = (row[0:1, :] * 64.0 + row[1:2, :] - 64.0).astype(i32)
    outs = []
    for i in range(8):
        rows = slice(i * 256, i * 256 + 256)
        mask = iota((256, 512), 0) + i * 256 == leader
        hit = jnp.max(jnp.where(mask, 1.0, 0.0), axis=1, keepdims=True)
        new = dot(hot(mask), joint[512:1024, :])
        moved[rows, :] = jnp.where(hit > 0.0, new, memory[rows, :].astype(f32)).astype(bf16)
        rows = pl.ds(i * 256, 256)
        out = pltpu.make_async_copy(moved.at[rows], new_hbm.at[rows], out_sem.at[i])
        out.start()
        outs.append(out)
    emb_copy.wait()
    for out in outs:
        out.wait()


def per_device(
    memory,
    touched,
    src_pos,
    dst_owner,
    dst_slot,
    neighbors,
    ev_time,
    neigh_time,
    time_freq,
    w_query,
    w_key,
    w_value,
    w_out,
    w_msg1,
    w_msg2,
    w_input,
    w_hidden,
):
    vmem = pl.BlockSpec(memory_space=pltpu.VMEM)
    anyw = pl.BlockSpec(memory_space=pl.ANY)
    weights = (w_hidden, w_query, w_key, w_value, w_out, w_msg1, w_msg2, w_input)

    def local(*shape, dtype=bf16):
        return pltpu.VMEM(shape, dtype)

    sems = pltpu.SemaphoreType.DMA
    joint = pl.pallas_call(
        window_kernel,
        out_shape=jax.ShapeDtypeStruct((1040, 512), bf16),
        in_specs=[vmem] * 8 + [anyw] * 9,
        out_specs=anyw,
        scratch_shapes=[
            local(*memory.shape),
            *[local(*w.shape) for w in weights],
            sems((9,)),
            sems,
            sems,
            local(40, 512, dtype=i32),
            local(128, 128, dtype=i32),
            local(128, 1, 128, dtype=i32),
            local(128, 1, 128, dtype=i32),
            sems((2,)),
            sems((5,)),
            local(2048, 128, dtype=f32),
            local(128, 16, 128),
            local(128, 16, 128),
            sems((2,)),
            local(2, 128, 16, 128),
            local(2, 128, 16, 128),
            sems((4,)),
            local(16, 128, 512, dtype=f32),
            local(512, 512),
            local(512, 1536, dtype=f32),
            local(512, 640),
            local(512, 512),
            local(512, 128, dtype=f32),
            local(512, 128),
            local(512, 512),
            local(512, 512),
            local(512, 512),
            local(512, 512),
            local(2, 512, 512, dtype=f32),
            local(2, 128, 512, dtype=f32),
            local(2, 640, 512),
            local(2, 640, 512),
            local(512, 512),
            local(512, 512),
            local(512, 1536, dtype=f32),
            local(16, 512),
            sems,
            local(512, 512),
            local(512, 512, dtype=i32),
            *[local(512, 512)] * 4,
            local(512, 640),
            local(512, 512),
            local(512, 1024, dtype=f32),
        ],
        compiler_params=pltpu.CompilerParams(
            collective_id=0, has_side_effects=True, vmem_limit_bytes=58 << 20
        ),
        name="window",
    )(
        touched.transpose(0, 2, 1),
        src_pos[None, :],
        dst_owner.reshape(1, -1),
        dst_slot[None, :],
        neighbors.T,
        ev_time[None, :],
        neigh_time.T,
        time_freq[None, :],
        memory,
        *weights,
    )
    return pl.pallas_call(
        place_kernel,
        out_shape=(
            jax.ShapeDtypeStruct((512, 512), bf16),
            jax.ShapeDtypeStruct(memory.shape, bf16),
        ),
        in_specs=[vmem, vmem],
        out_specs=(anyw, anyw),
        scratch_shapes=[local(*memory.shape), sems, sems((8,))],
        compiler_params=pltpu.CompilerParams(vmem_limit_bytes=12 << 20),
        name="place",
    )(joint, memory)


def solution(mesh):
    rows = P(("owner", "group"))
    in_specs = (rows,) * 8 + (P(),) * 9
    return jax.shard_map(
        per_device, mesh=mesh, in_specs=in_specs, out_specs=(rows, rows), check_vma=False
    )
```

```python
import jax
import jax.numpy as jnp
from jax import lax
from jax.experimental import pallas as pl
from jax.experimental.pallas import tpu as pltpu
from jax.sharding import PartitionSpec as P

HEADS = 2
MESH = pl.DeviceIdType.MESH
f32, bf16, i32 = jnp.float32, jnp.bfloat16, jnp.int32
COS = (
    0.9999992251396179,
    -0.499994158744812,
    0.041659727692604065,
    -0.00138586456887424,
    2.4201255655498244e-05,
    -2.196603787751883e-07,
)
NN = (((1,), (0,)), ((), ()))
NT = (((1,), (1,)), ((), ()))


def dot(a, b, dims=NN):
    return lax.dot_general(a, b, dims, preferred_element_type=f32)


def iota(shape, axis):
    return lax.broadcasted_iota(i32, shape, axis)


def hot(mask):
    return jnp.where(mask, 1.0, 0.0).astype(bf16)


def split(x):
    high = x.astype(bf16)
    return high, (x - high.astype(f32)).astype(bf16)


def take(x, index):
    return jnp.take_along_axis(x, index, axis=0, mode="promise_in_bounds")


def cosine(x):
    turns = jnp.floor(x * 0.15915494309189535 + 0.5)
    r = (x - turns * 6.28125) - turns * 0.0019353071795864769
    r = r * r
    y = COS[-1] * r + COS[-2]
    for c in COS[-3::-1]:
        y = y * r + c
    return y


def window_kernel(
    touched,
    src_pos,
    dst_owner,
    dst_slot,
    neighbors,
    ev_time,
    neigh_time,
    time_freq,
    memory_hbm,
    w_hidden_hbm,
    w_query_hbm,
    w_key_hbm,
    w_value_hbm,
    w_out_hbm,
    w_msg1_hbm,
    w_msg2_hbm,
    w_input_hbm,
    joint_hbm,
    memory,
    w_hidden,
    w_query,
    w_key,
    w_value,
    w_out,
    w_msg1,
    w_msg2,
    w_input,
    load_sem,
    emb_sem,
    new_sem,
    ints,
    natural,
    note,
    notes,
    note_sem,
    own_sem,
    stage,
    outbox,
    inbox,
    table_sem,
    part_out,
    part_in,
    part_sem,
    code,
    picked,
    state,
    value_t,
    match_ref,
    share,
    ev_code,
    src_hot,
    dst_hot,
    dst_hot_t,
    table,
    full,
    query_code,
    spread_hi,
    spread_lo,
    emb,
    partial,
    gates,
    lead,
    lead_sem,
    fresh,
    finder,
    query_hi,
    query_lo,
    key_hi,
    key_lo,
    value_hi,
    value_lo,
    before,
    scale,
):
    groups, owners = 8, 16
    n = groups * owners
    o, g = lax.axis_index("owner"), lax.axis_index("group")
    me = o * groups + g
    neigh, te, width = 16, 128, 512

    barrier = pltpu.get_barrier_semaphore()

    def greet(step, carry):
        peer = (me + step) & (n - 1)
        pl.semaphore_signal(
            barrier,
            inc=1,
            device_id=(peer // groups, peer & (groups - 1)),
            device_id_type=MESH,
        )
        return carry

    lax.fori_loop(1, n, greet, 0)
    loads = []
    for number, (source, target) in enumerate(
        (
            (memory_hbm, memory),
            (w_hidden_hbm, w_hidden),
            (w_value_hbm, w_value),
            (w_query_hbm, w_query),
            (w_key_hbm, w_key),
            (w_out_hbm, w_out),
            (w_msg1_hbm, w_msg1),
            (w_msg2_hbm, w_msg2),
            (w_input_hbm, w_input),
        )
    ):
        load = pltpu.make_async_copy(source, target, load_sem.at[number])
        load.start()
        loads.append(load)

    ints[0:neigh, :] = neighbors[...]
    ints[neigh : 2 * neigh, :] = ev_time[...] - neigh_time[...]
    ints[32:33, :] = src_pos[...]
    ints[33:34, :] = dst_owner[...] * 4 + dst_slot[...]
    ints[34:35, :] = ev_time[...]
    ints[35:40, :] = jnp.zeros((5, 512), i32)
    cols = ints[32:40, :].astype(f32).T.astype(i32)
    freq_row = time_freq[...]
    freq_col = jnp.broadcast_to(freq_row, (8, te)).T[:, 0:1]

    owner_hot = hot(iota((n, 512), 0) == dst_owner[...])
    slot_hot = hot(iota((n, 512), 0) == dst_slot[...] + 4)
    natural[...] = dot(owner_hot, slot_hot, NT).astype(i32)
    wanted = jnp.concatenate([touched[0], touched[0]], axis=0).astype(f32)
    natural[:, 0:4] = wanted.T[:, 0:4].astype(i32)
    note[:, 0, :] = natural[...]
    pl.semaphore_wait(barrier, n - 1)

    def send_all(source, target, send_sem, recv_sem):
        def send(step, carry):
            peer = (me + step) & (n - 1)
            pltpu.make_async_remote_copy(
                src_ref=source.at[peer],
                dst_ref=target.at[me],
                send_sem=send_sem,
                recv_sem=recv_sem,
                device_id=(peer // groups, peer & (groups - 1)),
                device_id_type=MESH,
            ).start()
            return carry

        lax.fori_loop(1, n, send, 0)

    def all_sent(source, target, send_sem, recv_sem):
        return pltpu.make_async_remote_copy(
            src_ref=source.at[pl.ds(0, n - 1)],
            dst_ref=target.at[pl.ds(0, n - 1)],
            send_sem=send_sem,
            recv_sem=recv_sem,
            device_id=(o, (g + 1) & (groups - 1)),
            device_id_type=MESH,
        )

    own = pltpu.make_async_copy(note.at[me], notes.at[me], own_sem.at[0])
    own.start()
    send_all(note, notes, note_sem.at[0], note_sem.at[1])

    def make_codes(first):
        def codes(k, carry):
            for i in range(te // 32):
                rows = slice(i * 32, i * 32 + 32)
                code[k, rows, :] = cosine(freq_col[rows] * delta).astype(bf16).astype(f32)
            return carry

        for k in range(first, first + neigh // 2):
            delta = ints[k + neigh : k + neigh + 1, :].astype(f32)
            codes(k, 0)

    make_codes(0)
    make_codes(neigh // 2)

    def find(piece, carry):
        lanes = pl.ds(pl.multiple_of(piece * 128, 128), 128)
        near = ints[0:neigh, lanes]
        near8 = [jnp.broadcast_to(near[k : k + 1, :], (8, 128)) for k in range(neigh)]
        sub = iota((8, 128), 0)

        def scan(i, carry):
            for u in range(4):
                base = pl.multiple_of(i * 32 + u * 8, 8)
                which = jnp.full((8, 128), neigh, i32)
                for k in range(neigh):
                    which = jnp.where(sub + base == near8[k], k, which)
                finder[pl.ds(base, 8), lanes] = which
            return carry

        lax.fori_loop(0, 16, scan, 0)
        return carry

    lax.fori_loop(0, 4, find, 0)
    own.wait()
    all_sent(note, notes, note_sem.at[0], note_sem.at[1]).wait()
    known = notes[:, 0, :]
    known_t = known.astype(f32).T.astype(i32)

    loads[0].wait()
    for s in range(4):
        rows = dot(hot(iota((n, 2048), 1) == known[:, s : s + 1]), memory[...])
        picked[s * n : (s + 1) * n, :] = rows.astype(bf16)
        for c in range(4):
            stage[pl.ds(s * 4 + c, n, stride=16), :] = rows[:, c * 128 : (c + 1) * 128]
    outbox[...] = stage[...].astype(bf16).reshape(n, 16, 128)

    own = pltpu.make_async_copy(outbox.at[me], inbox.at[me], own_sem.at[2])
    own.start()
    send_all(outbox, inbox, table_sem.at[0], table_sem.at[1])

    loads[1].wait()
    state[...] = dot(picked[...], w_hidden[...])
    loads[2].wait()
    value_t[...] = w_value[...].astype(f32).T.astype(bf16)
    value_hi[:, width:] = value_t[:, width:]
    asked_col = jnp.concatenate([known[:, s : s + 1] for s in range(4)], axis=0)
    count_col = jnp.concatenate([known[:, s + 4 : s + 5] for s in range(4)], axis=0)
    asked_row = jnp.concatenate([known_t[s : s + 1, :] for s in range(4)], axis=1)
    count_row = jnp.concatenate([known_t[s + 4 : s + 5, :] for s in range(4)], axis=1)
    match = asked_col == asked_row
    match_ref[...] = hot(match)
    number = jnp.sum(jnp.where(match, count_row.astype(f32), 0.0), axis=1, keepdims=True)
    share[...] = jnp.broadcast_to(1.0 / jnp.maximum(number, 1.0), share.shape)
    number_row = jnp.sum(jnp.where(match, count_col.astype(f32), 0.0), axis=0, keepdims=True)
    earlier = match & (iota((512, 512), 0) < iota((512, 512), 1))
    earlier = jnp.sum(jnp.where(earlier, 1.0, 0.0), axis=0, keepdims=True)
    leader = jnp.where((earlier == 0.0) & (number_row > 0.0), asked_row, -1)
    row = jnp.broadcast_to(leader + 64, lead.shape)
    row = jnp.where(iota(lead.shape, 0) == 0, row >> 6, row & 63)
    lead[...] = row.astype(f32).astype(bf16)
    lead_copy = pltpu.make_async_copy(lead, joint_hbm.at[pl.ds(1024, 16)], lead_sem)
    lead_copy.start()
    ev_code[...] = cosine(cols[:, 2:3].astype(f32) * freq_row).astype(bf16)
    src_hot[...] = hot(iota((512, 512), 1) == cols[:, 0:1])
    dst_hot[...] = hot(iota((512, 512), 1) == cols[:, 1:2])
    dst_hot_t[...] = hot(iota((512, 512), 0) == ints[33:34, :])

    own.wait()
    all_sent(outbox, inbox, table_sem.at[0], table_sem.at[1]).wait()
    stage[...] = inbox[...].reshape(n * 16, 128).astype(f32)
    for c in range(4):
        table[:, c * 128 : (c + 1) * 128] = stage[pl.ds(c, 512, stride=4), :].astype(bf16)

    dst_mem = dot(dst_hot[...], table[...])
    loads[3].wait()
    loads[4].wait()
    query = dot(dst_mem.astype(bf16), w_query[...]) * (1.0 / 16.0)
    query_hi[...], query_lo[...] = split(query)
    key_hi[...], key_lo[...] = split(dot(table[...], w_key[:width, :]))
    for h in range(HEADS):
        part = slice(h * 256, h * 256 + 256)
        query_code[h] = dot(w_key[width:, part], query_hi[:, part], NT) + dot(
            w_key[width:, part], query_lo[:, part], NT
        )
        full[h] = (
            dot(key_hi[:, part], query_hi[:, part], NT)
            + dot(key_hi[:, part], query_lo[:, part], NT)
            + dot(key_lo[:, part], query_hi[:, part], NT)
        )
    loads[6].wait()

    def attend(piece, carry):
        lanes = pl.ds(pl.multiple_of(piece * 128, 128), 128)
        value_hi[lanes, :width], value_lo[lanes, :] = split(
            dot(value_t[lanes, :width], table[...], NT)
        )
        src_mem = dot(src_hot[lanes, :], table[...]).astype(bf16)
        before[lanes, :] = dot(src_mem, w_msg1[:width, :]) + dot(
            ev_code[lanes, :], w_msg1[2 * width :, :]
        )
        near = ints[0:neigh, lanes]
        fine = [near[b * 8 : b * 8 + 8, :] & 7 for b in range(2)]
        coarse = [near[b * 8 : b * 8 + 8, :] >> 3 for b in range(2)]

        zero = jnp.zeros((8, 128), f32)
        def timed(i, sums):
            sums = list(sums)
            rows = pl.ds(pl.multiple_of(i * 8, 8), 8)
            mine = [query_code[h, rows, lanes] for h in range(HEADS)]
            for k in range(neigh):
                one = code[k, rows, lanes]
                for h in range(HEADS):
                    sums[h * neigh + k] += one * mine[h]
            return tuple(sums)

        sums = lax.fori_loop(0, te // 8, timed, (zero,) * (HEADS * neigh), unroll=16)
        def look(i, found):
            found = list(found)
            for u in range(8):
                base = pl.multiple_of(i * 64 + u * 8, 8)
                for b in range(2):
                    mask = coarse[b] == i * 8 + u
                    for h in range(HEADS):
                        taken = take(full[h, pl.ds(base, 8), lanes], fine[b])
                        found[h * 2 + b] = jnp.where(mask, taken, found[h * 2 + b])
            return tuple(found)

        found = lax.fori_loop(0, 8, look, (zero,) * (2 * HEADS), unroll=8)

        whole = []
        weights = []
        for h in range(HEADS):
            score = jnp.concatenate(
                [
                    jnp.sum(sums[h * neigh + k], axis=0, keepdims=True)
                    for k in range(neigh)
                ],
                axis=0,
            ) + jnp.concatenate(found[h * 2 : h * 2 + 2], axis=0)
            score = jnp.exp(score - jnp.max(score, axis=0, keepdims=True))
            weight = score.astype(bf16).astype(f32)
            scale[h : h + 1, lanes] = 1.0 / jnp.sum(weight, axis=0, keepdims=True)
            total = jnp.zeros((neigh, 128), f32)
            for k in range(neigh):
                total += jnp.where(near == near[k : k + 1, :], weight[k : k + 1, :], 0.0)
            weights.append(weight)
            whole.append([total[0:8, :], total[8:16, :]])

        def put(i, carry):
            for u in range(4):
                base = pl.multiple_of(i * 64 + u * 16, 16)
                both = [[], []]
                for v in range(2):
                    which = finder[pl.ds(base + v * 8, 8), lanes]
                    fine = which & 7
                    for h in range(HEADS):
                        first = jnp.where(which < 8, take(whole[h][0], fine), 0.0)
                        second = take(whole[h][1], fine)
                        both[h].append(
                            jnp.where((which & 24) == 8, second, first)
                        )
                for h in range(HEADS):
                    spread_hi[h, pl.ds(base, 16), lanes] = jnp.concatenate(
                        both[h], axis=0
                    ).astype(bf16)
            return carry

        lax.fori_loop(0, 8, put, 0, unroll=8)
        spread = [
            [jnp.broadcast_to(weights[h][k : k + 1, :], (8, 128)) for k in range(neigh)]
            for h in range(HEADS)
        ]

        def mix(i, carry):
            base = pl.multiple_of(i * 16, 16)
            both = [[], []]
            for v in range(2):
                mixed = [zero] * HEADS
                for k in range(neigh):
                    one = code[k, pl.ds(base + v * 8, 8), lanes]
                    for h in range(HEADS):
                        mixed[h] += one * spread[h][k]
                for h in range(HEADS):
                    both[h].append(mixed[h])
            for h in range(HEADS):
                high, low = split(jnp.concatenate(both[h], axis=0))
                spread_hi[h, pl.ds(width + base, 16), lanes] = high
                spread_lo[h, pl.ds(base, 16), lanes] = low
            return carry

        lax.fori_loop(0, te // 16, mix, 0, unroll=8)
        return carry

    lax.fori_loop(0, 4, attend, 0, unroll=2)
    att = []
    for h in range(HEADS):
        part = slice(h * 256, h * 256 + 256)
        att.append(
            (
                dot(value_hi[part, :], spread_hi[h])
                + dot(value_hi[part, width:], spread_lo[h])
                + dot(value_lo[part, :], spread_hi[h, :width, :])
            )
            * scale[h : h + 1, :]
        )
    att = jnp.concatenate(att, axis=0).T.astype(bf16)
    loads[5].wait()
    emb[...] = (dst_mem + dot(att, w_out[...])).astype(bf16)
    emb_copy = pltpu.make_async_copy(emb, joint_hbm.at[pl.ds(0, 512)], emb_sem)
    emb_copy.start()
    hidden = before[...] + dot(emb[...], w_msg1[width : 2 * width, :])
    hidden = jnp.maximum(hidden, 0.0).astype(bf16)
    loads[7].wait()
    owns = []
    for half in range(2):
        part = slice(half * 512, half * 512 + 512)
        message = dot(hidden, w_msg2[:, part]).astype(bf16)
        sums = dot(dst_hot_t[...], message)
        for c in range(4):
            stage[pl.ds(c, 512, stride=4), :] = sums[:, c * 128 : (c + 1) * 128]
        part_out[half] = stage[...].astype(bf16).reshape(n, 16, 128)
        own = pltpu.make_async_copy(
            part_out.at[half, me], part_in.at[half, me], own_sem.at[3 + half]
        )
        own.start()
        owns.append(own)
        send_all(
            part_out.at[half], part_in.at[half], part_sem.at[2 * half], part_sem.at[2 * half + 1]
        )
    emb_copy.wait()
    loads[8].wait()
    for half in range(2):
        owns[half].wait()
        all_sent(
            part_out.at[half], part_in.at[half], part_sem.at[2 * half], part_sem.at[2 * half + 1]
        ).wait()
        stage[...] = part_in[half].reshape(n * 16, 128).astype(f32)
        for s in range(4):
            for c in range(4):
                partial[s * n : (s + 1) * n, c * 128 : (c + 1) * 128] = stage[
                    pl.ds(s * 4 + c, n, stride=16), :
                ].astype(bf16)
        total = dot(match_ref[...], partial[...])
        agg = jnp.concatenate(
            [total[:, c * 128 : (c + 1) * 128] * share[...] for c in range(4)], axis=1
        ).astype(bf16)
        gate = dot(agg, w_input[half * 512 : half * 512 + 512, :])
        if half == 0:
            gates[...] = gate
        else:
            gates[...] += gate

    def update_rows(i, carry):
        rows = pl.ds(pl.multiple_of(i * 64, 64), 64)
        reset = jax.nn.sigmoid(gates[rows, 0:width] + state[rows, 0:width])
        update = jax.nn.sigmoid(
            gates[rows, width : 2 * width] + state[rows, width : 2 * width]
        )
        new = jnp.tanh(gates[rows, 2 * width :] + reset * state[rows, 2 * width :])
        old = picked[rows, :].astype(f32)
        fresh[rows, :] = ((1.0 - update) * new + update * old).astype(bf16)
        return carry

    lax.fori_loop(0, 8, update_rows, 0)

    fresh_copy = pltpu.make_async_copy(fresh, joint_hbm.at[pl.ds(512, 512)], new_sem)
    fresh_copy.start()
    lead_copy.wait()
    fresh_copy.wait()


def place_kernel(joint, memory, emb_out, new_hbm, moved, emb_sem, out_sem):
    emb_copy = pltpu.make_async_copy(joint.at[pl.ds(0, 512)], emb_out, emb_sem)
    emb_copy.start()
    row = joint[1024:1040, :].astype(f32)
    leader = (row[0:1, :] * 64.0 + row[1:2, :] - 64.0).astype(i32)
    outs = []
    for i in range(8):
        rows = slice(i * 256, i * 256 + 256)
        mask = iota((256, 512), 0) + i * 256 == leader
        hit = jnp.max(jnp.where(mask, 1.0, 0.0), axis=1, keepdims=True)
        new = dot(hot(mask), joint[512:1024, :])
        moved[rows, :] = jnp.where(hit > 0.0, new, memory[rows, :].astype(f32)).astype(bf16)
        rows = pl.ds(i * 256, 256)
        out = pltpu.make_async_copy(moved.at[rows], new_hbm.at[rows], out_sem.at[i])
        out.start()
        outs.append(out)
    emb_copy.wait()
    for out in outs:
        out.wait()


def per_device(
    memory,
    touched,
    src_pos,
    dst_owner,
    dst_slot,
    neighbors,
    ev_time,
    neigh_time,
    time_freq,
    w_query,
    w_key,
    w_value,
    w_out,
    w_msg1,
    w_msg2,
    w_input,
    w_hidden,
):
    vmem = pl.BlockSpec(memory_space=pltpu.VMEM)
    anyw = pl.BlockSpec(memory_space=pl.ANY)
    weights = (w_hidden, w_query, w_key, w_value, w_out, w_msg1, w_msg2, w_input)

    def local(*shape, dtype=bf16):
        return pltpu.VMEM(shape, dtype)

    sems = pltpu.SemaphoreType.DMA
    joint = pl.pallas_call(
        window_kernel,
        out_shape=jax.ShapeDtypeStruct((1040, 512), bf16),
        in_specs=[vmem] * 8 + [anyw] * 9,
        out_specs=anyw,
        scratch_shapes=[
            local(*memory.shape),
            *[local(*w.shape) for w in weights],
            sems((9,)),
            sems,
            sems,
            local(40, 512, dtype=i32),
            local(128, 128, dtype=i32),
            local(128, 1, 128, dtype=i32),
            local(128, 1, 128, dtype=i32),
            sems((2,)),
            sems((5,)),
            local(2048, 128, dtype=f32),
            local(128, 16, 128),
            local(128, 16, 128),
            sems((2,)),
            local(2, 128, 16, 128),
            local(2, 128, 16, 128),
            sems((4,)),
            local(16, 128, 512, dtype=f32),
            local(512, 512),
            local(512, 1536, dtype=f32),
            local(512, 640),
            local(512, 512),
            local(512, 128, dtype=f32),
            local(512, 128),
            local(512, 512),
            local(512, 512),
            local(512, 512),
            local(512, 512),
            local(2, 512, 512, dtype=f32),
            local(2, 128, 512, dtype=f32),
            local(2, 640, 512),
            local(2, 128, 512),
            local(512, 512),
            local(512, 512),
            local(512, 1536, dtype=f32),
            local(16, 512),
            sems,
            local(512, 512),
            local(512, 512, dtype=i32),
            *[local(512, 512)] * 4,
            local(512, 640),
            local(512, 512),
            local(512, 1024, dtype=f32),
            local(8, 512, dtype=f32),
        ],
        compiler_params=pltpu.CompilerParams(
            collective_id=0, has_side_effects=True, vmem_limit_bytes=58 << 20
        ),
        name="window",
    )(
        touched.transpose(0, 2, 1),
        src_pos[None, :],
        dst_owner.reshape(1, -1),
        dst_slot[None, :],
        neighbors.T,
        ev_time[None, :],
        neigh_time.T,
        time_freq[None, :],
        memory,
        *weights,
    )
    return pl.pallas_call(
        place_kernel,
        out_shape=(
            jax.ShapeDtypeStruct((512, 512), bf16),
            jax.ShapeDtypeStruct(memory.shape, bf16),
        ),
        in_specs=[vmem, vmem],
        out_specs=(anyw, anyw),
        scratch_shapes=[local(*memory.shape), sems, sems((8,))],
        compiler_params=pltpu.CompilerParams(vmem_limit_bytes=12 << 20),
        name="place",
    )(joint, memory)


def solution(mesh):
    rows = P(("owner", "group"))
    in_specs = (rows,) * 8 + (P(),) * 9
    return jax.shard_map(
        per_device, mesh=mesh, in_specs=in_specs, out_specs=(rows, rows), check_vma=False
    )
```

```python
import jax
import jax.numpy as jnp
from jax import lax
from jax.experimental import pallas as pl
from jax.experimental.pallas import tpu as pltpu
from jax.sharding import PartitionSpec as P

HEADS = 2
MESH = pl.DeviceIdType.MESH
f32, bf16, i32 = jnp.float32, jnp.bfloat16, jnp.int32
COS = (
    0.9999992251396179,
    -0.499994158744812,
    0.041659727692604065,
    -0.00138586456887424,
    2.4201255655498244e-05,
    -2.196603787751883e-07,
)
NN = (((1,), (0,)), ((), ()))
NT = (((1,), (1,)), ((), ()))


def dot(a, b, dims=NN):
    return lax.dot_general(a, b, dims, preferred_element_type=f32)


def iota(shape, axis):
    return lax.broadcasted_iota(i32, shape, axis)


def hot(mask):
    return jnp.where(mask, 1.0, 0.0).astype(bf16)


def split(x):
    high = x.astype(bf16)
    return high, (x - high.astype(f32)).astype(bf16)


def take(x, index):
    return jnp.take_along_axis(x, index, axis=0, mode="promise_in_bounds")


def cosine(x):
    turns = jnp.floor(x * 0.15915494309189535 + 0.5)
    r = (x - turns * 6.28125) - turns * 0.0019353071795864769
    r = r * r
    y = COS[-1] * r + COS[-2]
    for c in COS[-3::-1]:
        y = y * r + c
    return y


def window_kernel(
    touched,
    src_pos,
    dst_owner,
    dst_slot,
    neighbors,
    ev_time,
    neigh_time,
    time_freq,
    memory_hbm,
    w_hidden_hbm,
    w_query_hbm,
    w_key_hbm,
    w_value_hbm,
    w_out_hbm,
    w_msg1_hbm,
    w_msg2_hbm,
    w_input_hbm,
    joint_hbm,
    memory,
    w_hidden,
    w_query,
    w_key,
    w_value,
    w_out,
    w_msg1,
    w_msg2,
    w_input,
    load_sem,
    emb_sem,
    new_sem,
    ints,
    natural,
    note,
    notes,
    note_sem,
    own_sem,
    stage,
    outbox,
    inbox,
    table_sem,
    part_out,
    part_in,
    part_sem,
    code,
    picked,
    state,
    value_t,
    match_ref,
    share,
    ev_code,
    src_hot,
    dst_hot,
    dst_hot_t,
    table,
    full,
    query_code,
    spread_hi,
    spread_lo,
    emb,
    partial,
    gates,
    lead,
    lead_sem,
    fresh,
    finder,
    query_hi,
    query_lo,
    key_hi,
    key_lo,
    value_hi,
    value_lo,
    before,
    scale,
):
    groups, owners = 8, 16
    n = groups * owners
    o, g = lax.axis_index("owner"), lax.axis_index("group")
    me = o * groups + g
    neigh, te, width = 16, 128, 512

    barrier = pltpu.get_barrier_semaphore()

    def greet(step, carry):
        peer = (me + step) & (n - 1)
        pl.semaphore_signal(
            barrier,
            inc=1,
            device_id=(peer // groups, peer & (groups - 1)),
            device_id_type=MESH,
        )
        return carry

    lax.fori_loop(1, n, greet, 0)
    loads = []
    for number, (source, target) in enumerate(
        (
            (memory_hbm, memory),
            (w_hidden_hbm, w_hidden),
            (w_value_hbm, w_value),
            (w_query_hbm, w_query),
            (w_key_hbm, w_key),
            (w_out_hbm, w_out),
            (w_msg1_hbm, w_msg1),
            (w_msg2_hbm, w_msg2),
            (w_input_hbm, w_input),
        )
    ):
        load = pltpu.make_async_copy(source, target, load_sem.at[number])
        load.start()
        loads.append(load)

    ints[0:neigh, :] = neighbors[...]
    ints[neigh : 2 * neigh, :] = ev_time[...] - neigh_time[...]
    ints[32:33, :] = src_pos[...]
    ints[33:34, :] = dst_owner[...] * 4 + dst_slot[...]
    ints[34:35, :] = ev_time[...]
    ints[35:40, :] = jnp.zeros((5, 512), i32)
    cols = ints[32:40, :].astype(f32).T.astype(i32)
    freq_row = time_freq[...]
    freq_col = jnp.broadcast_to(freq_row, (8, te)).T[:, 0:1]

    owner_hot = hot(iota((n, 512), 0) == dst_owner[...])
    slot_hot = hot(iota((n, 512), 0) == dst_slot[...] + 4)
    natural[...] = dot(owner_hot, slot_hot, NT).astype(i32)
    wanted = jnp.concatenate([touched[0], touched[0]], axis=0).astype(f32)
    natural[:, 0:4] = wanted.T[:, 0:4].astype(i32)
    note[:, 0, :] = natural[...]
    pl.semaphore_wait(barrier, n - 1)

    def send_all(source, target, send_sem, recv_sem):
        def send(step, carry):
            peer = (me + step) & (n - 1)
            pltpu.make_async_remote_copy(
                src_ref=source.at[peer],
                dst_ref=target.at[me],
                send_sem=send_sem,
                recv_sem=recv_sem,
                device_id=(peer // groups, peer & (groups - 1)),
                device_id_type=MESH,
            ).start()
            return carry

        lax.fori_loop(1, n, send, 0)

    def all_sent(source, target, send_sem, recv_sem):
        return pltpu.make_async_remote_copy(
            src_ref=source.at[pl.ds(0, n - 1)],
            dst_ref=target.at[pl.ds(0, n - 1)],
            send_sem=send_sem,
            recv_sem=recv_sem,
            device_id=(o, (g + 1) & (groups - 1)),
            device_id_type=MESH,
        )

    own = pltpu.make_async_copy(note.at[me], notes.at[me], own_sem.at[0])
    own.start()
    send_all(note, notes, note_sem.at[0], note_sem.at[1])

    def make_codes(first):
        def codes(k, carry):
            for i in range(te // 32):
                rows = slice(i * 32, i * 32 + 32)
                code[k, rows, :] = cosine(freq_col[rows] * delta).astype(bf16).astype(f32)
            return carry

        for k in range(first, first + neigh // 2):
            delta = ints[k + neigh : k + neigh + 1, :].astype(f32)
            codes(k, 0)

    make_codes(0)
    make_codes(neigh // 2)

    def find(piece, carry):
        lanes = pl.ds(pl.multiple_of(piece * 128, 128), 128)
        near = ints[0:neigh, lanes]
        near8 = [jnp.broadcast_to(near[k : k + 1, :], (8, 128)) for k in range(neigh)]
        sub = iota((8, 128), 0)

        def scan(i, carry):
            for u in range(4):
                base = pl.multiple_of(i * 32 + u * 8, 8)
                which = jnp.full((8, 128), neigh, i32)
                for k in range(neigh):
                    which = jnp.where(sub + base == near8[k], k, which)
                finder[pl.ds(base, 8), lanes] = which
            return carry

        lax.fori_loop(0, 16, scan, 0)
        return carry

    lax.fori_loop(0, 4, find, 0)
    own.wait()
    all_sent(note, notes, note_sem.at[0], note_sem.at[1]).wait()
    known = notes[:, 0, :]
    known_t = known.astype(f32).T.astype(i32)

    loads[0].wait()
    asked_col = jnp.concatenate([known[:, s : s + 1] for s in range(4)], axis=0)
    rows = dot(hot(iota((512, 2048), 1) == asked_col), memory[...])
    picked[...] = rows.astype(bf16)
    for s in range(4):
        for c in range(4):
            stage[pl.ds(s * 4 + c, n, stride=16), :] = rows[
                s * n : (s + 1) * n, c * 128 : (c + 1) * 128
            ]
    outbox[...] = stage[...].astype(bf16).reshape(n, 16, 128)

    own = pltpu.make_async_copy(outbox.at[me], inbox.at[me], own_sem.at[2])
    own.start()
    send_all(outbox, inbox, table_sem.at[0], table_sem.at[1])

    loads[1].wait()
    state[...] = dot(picked[...], w_hidden[...])
    loads[2].wait()
    value_t[...] = w_value[...].astype(f32).T.astype(bf16)
    value_hi[:, width:] = value_t[:, width:]
    count_col = jnp.concatenate([known[:, s + 4 : s + 5] for s in range(4)], axis=0)
    asked_row = jnp.concatenate([known_t[s : s + 1, :] for s in range(4)], axis=1)
    count_row = jnp.concatenate([known_t[s + 4 : s + 5, :] for s in range(4)], axis=1)
    match = asked_col == asked_row
    match_ref[...] = hot(match)
    number = jnp.sum(jnp.where(match, count_row.astype(f32), 0.0), axis=1, keepdims=True)
    share[...] = jnp.broadcast_to(1.0 / jnp.maximum(number, 1.0), share.shape)
    number_row = jnp.sum(jnp.where(match, count_col.astype(f32), 0.0), axis=0, keepdims=True)
    earlier = match & (iota((512, 512), 0) < iota((512, 512), 1))
    earlier = jnp.sum(jnp.where(earlier, 1.0, 0.0), axis=0, keepdims=True)
    leader = jnp.where((earlier == 0.0) & (number_row > 0.0), asked_row, -1)
    row = jnp.broadcast_to(leader + 64, lead.shape)
    row = jnp.where(iota(lead.shape, 0) == 0, row >> 6, row & 63)
    lead[...] = row.astype(f32).astype(bf16)
    lead_copy = pltpu.make_async_copy(lead, joint_hbm.at[pl.ds(1024, 16)], lead_sem)
    lead_copy.start()
    ev_code[...] = cosine(cols[:, 2:3].astype(f32) * freq_row).astype(bf16)
    src_hot[...] = hot(iota((512, 512), 1) == cols[:, 0:1])
    dst_hot[...] = hot(iota((512, 512), 1) == cols[:, 1:2])
    dst_hot_t[...] = hot(iota((512, 512), 0) == ints[33:34, :])

    own.wait()
    all_sent(outbox, inbox, table_sem.at[0], table_sem.at[1]).wait()
    stage[...] = inbox[...].reshape(n * 16, 128).astype(f32)
    for c in range(4):
        table[:, c * 128 : (c + 1) * 128] = stage[pl.ds(c, 512, stride=4), :].astype(bf16)

    dst_mem = dot(dst_hot[...], table[...])
    loads[3].wait()
    loads[4].wait()
    query = dot(dst_mem.astype(bf16), w_query[...]) * (1.0 / 16.0)
    query_hi[...], query_lo[...] = split(query)
    key_hi[...], key_lo[...] = split(dot(table[...], w_key[:width, :]))
    for h in range(HEADS):
        part = slice(h * 256, h * 256 + 256)
        query_code[h] = dot(w_key[width:, part], query_hi[:, part], NT) + dot(
            w_key[width:, part], query_lo[:, part], NT
        )
        full[h] = (
            dot(key_hi[:, part], query_hi[:, part], NT)
            + dot(key_hi[:, part], query_lo[:, part], NT)
            + dot(key_lo[:, part], query_hi[:, part], NT)
        )
    loads[6].wait()

    def attend(piece, carry):
        lanes = pl.ds(pl.multiple_of(piece * 128, 128), 128)
        value_hi[lanes, :width], value_lo[lanes, :] = split(
            dot(value_t[lanes, :width], table[...], NT)
        )
        src_mem = dot(src_hot[lanes, :], table[...]).astype(bf16)
        before[lanes, :] = dot(src_mem, w_msg1[:width, :]) + dot(
            ev_code[lanes, :], w_msg1[2 * width :, :]
        )
        near = ints[0:neigh, lanes]
        fine = [near[b * 8 : b * 8 + 8, :] & 7 for b in range(2)]
        coarse = [near[b * 8 : b * 8 + 8, :] >> 3 for b in range(2)]

        zero = jnp.zeros((8, 128), f32)
        def timed(i, sums):
            sums = list(sums)
            rows = pl.ds(pl.multiple_of(i * 8, 8), 8)
            mine = [query_code[h, rows, lanes] for h in range(HEADS)]
            for k in range(neigh):
                one = code[k, rows, lanes]
                for h in range(HEADS):
                    sums[h * neigh + k] += one * mine[h]
            return tuple(sums)

        sums = lax.fori_loop(0, te // 8, timed, (zero,) * (HEADS * neigh), unroll=16)
        def look(i, found):
            found = list(found)
            for u in range(8):
                base = pl.multiple_of(i * 64 + u * 8, 8)
                for b in range(2):
                    mask = coarse[b] == i * 8 + u
                    for h in range(HEADS):
                        taken = take(full[h, pl.ds(base, 8), lanes], fine[b])
                        found[h * 2 + b] = jnp.where(mask, taken, found[h * 2 + b])
            return tuple(found)

        found = lax.fori_loop(0, 8, look, (zero,) * (2 * HEADS), unroll=8)

        whole = []
        weights = []
        for h in range(HEADS):
            score = jnp.concatenate(
                [
                    jnp.sum(sums[h * neigh + k], axis=0, keepdims=True)
                    for k in range(neigh)
                ],
                axis=0,
            ) + jnp.concatenate(found[h * 2 : h * 2 + 2], axis=0)
            score = jnp.exp(score - jnp.max(score, axis=0, keepdims=True))
            weight = score.astype(bf16).astype(f32)
            scale[h : h + 1, lanes] = 1.0 / jnp.sum(weight, axis=0, keepdims=True)
            total = jnp.zeros((neigh, 128), f32)
            for k in range(neigh):
                total += jnp.where(near == near[k : k + 1, :], weight[k : k + 1, :], 0.0)
            weights.append(weight)
            whole.append([total[0:8, :], total[8:16, :]])

        def put(i, carry):
            for u in range(4):
                base = pl.multiple_of(i * 64 + u * 16, 16)
                both = [[], []]
                for v in range(2):
                    which = finder[pl.ds(base + v * 8, 8), lanes]
                    fine = which & 7
                    for h in range(HEADS):
                        first = jnp.where(which < 8, take(whole[h][0], fine), 0.0)
                        second = take(whole[h][1], fine)
                        both[h].append(
                            jnp.where((which & 24) == 8, second, first)
                        )
                for h in range(HEADS):
                    spread_hi[h, pl.ds(base, 16), lanes] = jnp.concatenate(
                        both[h], axis=0
                    ).astype(bf16)
            return carry

        lax.fori_loop(0, 8, put, 0, unroll=8)
        spread = [
            [jnp.broadcast_to(weights[h][k : k + 1, :], (8, 128)) for k in range(neigh)]
            for h in range(HEADS)
        ]

        def mix(i, carry):
            base = pl.multiple_of(i * 16, 16)
            both = [[], []]
            for v in range(2):
                mixed = [zero] * HEADS
                for k in range(neigh):
                    one = code[k, pl.ds(base + v * 8, 8), lanes]
                    for h in range(HEADS):
                        mixed[h] += one * spread[h][k]
                for h in range(HEADS):
                    both[h].append(mixed[h])
            for h in range(HEADS):
                high, low = split(jnp.concatenate(both[h], axis=0))
                spread_hi[h, pl.ds(width + base, 16), lanes] = high
                spread_lo[h, pl.ds(base, 16), lanes] = low
            return carry

        lax.fori_loop(0, te // 16, mix, 0, unroll=8)
        return carry

    lax.fori_loop(0, 4, attend, 0, unroll=2)
    att = []
    for h in range(HEADS):
        part = slice(h * 256, h * 256 + 256)
        att.append(
            (
                dot(value_hi[part, :], spread_hi[h])
                + dot(value_hi[part, width:], spread_lo[h])
                + dot(value_lo[part, :], spread_hi[h, :width, :])
            )
            * scale[h : h + 1, :]
        )
    att = jnp.concatenate(att, axis=0).T.astype(bf16)
    loads[5].wait()
    emb[...] = (dst_mem + dot(att, w_out[...])).astype(bf16)
    emb_copy = pltpu.make_async_copy(emb, joint_hbm.at[pl.ds(0, 512)], emb_sem)
    emb_copy.start()
    hidden = before[...] + dot(emb[...], w_msg1[width : 2 * width, :])
    hidden = jnp.maximum(hidden, 0.0).astype(bf16)
    loads[7].wait()
    owns = []
    for half in range(2):
        part = slice(half * 512, half * 512 + 512)
        message = dot(hidden, w_msg2[:, part]).astype(bf16)
        sums = dot(dst_hot_t[...], message)
        for c in range(4):
            stage[pl.ds(c, 512, stride=4), :] = sums[:, c * 128 : (c + 1) * 128]
        part_out[half] = stage[...].astype(bf16).reshape(n, 16, 128)
        own = pltpu.make_async_copy(
            part_out.at[half, me], part_in.at[half, me], own_sem.at[3 + half]
        )
        own.start()
        owns.append(own)
        send_all(
            part_out.at[half], part_in.at[half], part_sem.at[2 * half], part_sem.at[2 * half + 1]
        )
    emb_copy.wait()
    loads[8].wait()
    for half in range(2):
        owns[half].wait()
        all_sent(
            part_out.at[half], part_in.at[half], part_sem.at[2 * half], part_sem.at[2 * half + 1]
        ).wait()
        stage[...] = part_in[half].reshape(n * 16, 128).astype(f32)
        for s in range(4):
            for c in range(4):
                partial[s * n : (s + 1) * n, c * 128 : (c + 1) * 128] = stage[
                    pl.ds(s * 4 + c, n, stride=16), :
                ].astype(bf16)
        total = dot(match_ref[...], partial[...])
        agg = jnp.concatenate(
            [total[:, c * 128 : (c + 1) * 128] * share[...] for c in range(4)], axis=1
        ).astype(bf16)
        gate = dot(agg, w_input[half * 512 : half * 512 + 512, :])
        if half == 0:
            gates[...] = gate
        else:
            gates[...] += gate

    def update_rows(i, carry):
        rows = pl.ds(pl.multiple_of(i * 64, 64), 64)
        reset = jax.nn.sigmoid(gates[rows, 0:width] + state[rows, 0:width])
        update = jax.nn.sigmoid(
            gates[rows, width : 2 * width] + state[rows, width : 2 * width]
        )
        new = jnp.tanh(gates[rows, 2 * width :] + reset * state[rows, 2 * width :])
        old = picked[rows, :].astype(f32)
        fresh[rows, :] = ((1.0 - update) * new + update * old).astype(bf16)
        return carry

    lax.fori_loop(0, 8, update_rows, 0)

    fresh_copy = pltpu.make_async_copy(fresh, joint_hbm.at[pl.ds(512, 512)], new_sem)
    fresh_copy.start()
    lead_copy.wait()
    fresh_copy.wait()


def place_kernel(joint, memory, emb_out, new_hbm, moved, emb_sem, out_sem):
    emb_copy = pltpu.make_async_copy(joint.at[pl.ds(0, 512)], emb_out, emb_sem)
    emb_copy.start()
    row = joint[1024:1040, :].astype(f32)
    leader = (row[0:1, :] * 64.0 + row[1:2, :] - 64.0).astype(i32)
    outs = []
    for i in range(8):
        rows = slice(i * 256, i * 256 + 256)
        mask = iota((256, 512), 0) + i * 256 == leader
        hit = jnp.max(jnp.where(mask, 1.0, 0.0), axis=1, keepdims=True)
        new = dot(hot(mask), joint[512:1024, :])
        moved[rows, :] = jnp.where(hit > 0.0, new, memory[rows, :].astype(f32)).astype(bf16)
        rows = pl.ds(i * 256, 256)
        out = pltpu.make_async_copy(moved.at[rows], new_hbm.at[rows], out_sem.at[i])
        out.start()
        outs.append(out)
    emb_copy.wait()
    for out in outs:
        out.wait()


def per_device(
    memory,
    touched,
    src_pos,
    dst_owner,
    dst_slot,
    neighbors,
    ev_time,
    neigh_time,
    time_freq,
    w_query,
    w_key,
    w_value,
    w_out,
    w_msg1,
    w_msg2,
    w_input,
    w_hidden,
):
    vmem = pl.BlockSpec(memory_space=pltpu.VMEM)
    anyw = pl.BlockSpec(memory_space=pl.ANY)
    weights = (w_hidden, w_query, w_key, w_value, w_out, w_msg1, w_msg2, w_input)

    def local(*shape, dtype=bf16):
        return pltpu.VMEM(shape, dtype)

    sems = pltpu.SemaphoreType.DMA
    joint = pl.pallas_call(
        window_kernel,
        out_shape=jax.ShapeDtypeStruct((1040, 512), bf16),
        in_specs=[vmem] * 8 + [anyw] * 9,
        out_specs=anyw,
        scratch_shapes=[
            local(*memory.shape),
            *[local(*w.shape) for w in weights],
            sems((9,)),
            sems,
            sems,
            local(40, 512, dtype=i32),
            local(128, 128, dtype=i32),
            local(128, 1, 128, dtype=i32),
            local(128, 1, 128, dtype=i32),
            sems((2,)),
            sems((5,)),
            local(2048, 128, dtype=f32),
            local(128, 16, 128),
            local(128, 16, 128),
            sems((2,)),
            local(2, 128, 16, 128),
            local(2, 128, 16, 128),
            sems((4,)),
            local(16, 128, 512, dtype=f32),
            local(512, 512),
            local(512, 1536, dtype=f32),
            local(512, 640),
            local(512, 512),
            local(512, 128, dtype=f32),
            local(512, 128),
            local(512, 512),
            local(512, 512),
            local(512, 512),
            local(512, 512),
            local(2, 512, 512, dtype=f32),
            local(2, 128, 512, dtype=f32),
            local(2, 640, 512),
            local(2, 128, 512),
            local(512, 512),
            local(512, 512),
            local(512, 1536, dtype=f32),
            local(16, 512),
            sems,
            local(512, 512),
            local(512, 512, dtype=i32),
            *[local(512, 512)] * 4,
            local(512, 640),
            local(512, 512),
            local(512, 1024, dtype=f32),
            local(8, 512, dtype=f32),
        ],
        compiler_params=pltpu.CompilerParams(
            collective_id=0, has_side_effects=True, vmem_limit_bytes=58 << 20
        ),
        name="window",
    )(
        touched.transpose(0, 2, 1),
        src_pos[None, :],
        dst_owner.reshape(1, -1),
        dst_slot[None, :],
        neighbors.T,
        ev_time[None, :],
        neigh_time.T,
        time_freq[None, :],
        memory,
        *weights,
    )
    return pl.pallas_call(
        place_kernel,
        out_shape=(
            jax.ShapeDtypeStruct((512, 512), bf16),
            jax.ShapeDtypeStruct(memory.shape, bf16),
        ),
        in_specs=[vmem, vmem],
        out_specs=(anyw, anyw),
        scratch_shapes=[local(*memory.shape), sems, sems((8,))],
        compiler_params=pltpu.CompilerParams(vmem_limit_bytes=12 << 20),
        name="place",
    )(joint, memory)


def solution(mesh):
    rows = P(("owner", "group"))
    in_specs = (rows,) * 8 + (P(),) * 9
    return jax.shard_map(
        per_device, mesh=mesh, in_specs=in_specs, out_specs=(rows, rows), check_vma=False
    )
```
